32 devices in a mesh: ctx: 16 (over z, y, x), head: 2 (over core).
Axes of the slice: x: 2, y: 2, z: 4, core: 2. Of those that a mesh axis runs over, the one named last changes fastest.
Arguments:
- tokens: bfloat16 [16384, 2048], P('ctx', 'head'), may hold values from -6 to 6
- w_qkv: bfloat16 [3, 2048, 2048], P(None, 'ctx', 'head'), may hold values from -0.125 to 0.125
- out_gain: float32 [2048], P('head'), may hold values from 0.25 to 1.75
- seg_ids: int32 [16384], P('ctx'), may hold values from 0 to 15, never falling along the last dimension, each value on 1 to 4096 neighbouring positions
Outputs:
- attended: bfloat16 [16384, 2048], P('ctx', 'head')
The draws below stay inside these ranges and needn't reach their ends.
Inputs may be any that keep to these rules, and one draw needn't show every extreme that they name: `seg_ids`: segment numbers never fall along the stream; each segment covers 1 to 4096 consecutive tokens, and one covers exactly 4096.
All inputs are finite; a program needn't handle non-finite values.
Results may differ from the reference program's by a relative error of at most 0.012.
Values may be sent and summed in bfloat16 or wider, within the bound.
A program may use at most 64 MiB of HBM per device.

```python
import math
import jax
import jax.numpy as jnp
import numpy as np
from jax import lax

HEADS = 16
HEAD_DIM = 128
D = 2048
TOK_DEV = 1024
TOKENS = 16384
SEGS = 16
SPAN = 4096
N_CTX = 16


def block_levels(stream_key, extent, shards, least, largest):
    def one(position, parts):
        draws = jax.random.uniform(jax.random.fold_in(jax.random.fold_in(stream_key, 6), position), (parts,), jnp.float32, least / len(shards), largest / len(shards))
        return jnp.repeat(jnp.exp(draws), extent[position] // parts).reshape((-1,) + (1,) * (len(extent) - position - 1))

    loudness = one(*shards[0])
    for cut in shards[1:]:
        loudness = loudness * one(*cut)
    return loudness


def split_up(number_of, total, bound, lean):
    loads = [(1 << 20) // math.isqrt(standing ** lean) + 1 for standing in range(2, number_of + 1)]
    spare, holding = total - bound - (number_of - 1), [1] * (number_of - 1)
    while spare > 0:
        movable = [i for i in range(number_of - 1) if holding[i] < bound]
        pool, budget = sum([loads[i] for i in movable]), spare
        for i in movable:
            extra = min(bound - holding[i], max(1, budget * loads[i] // pool), spare)
            holding[i] = holding[i] + extra
            spare = spare - extra
    return np.array([bound] + holding)


def ragged_sizes(key, count, total, most, lean):
    if count == 2:
        one = jax.random.randint(key, (), max(1, total - most), min(most, total - 1) + 1)
        return jnp.stack([one, total - one])
    tallies = jnp.asarray(split_up(count, total, most, lean), jnp.int32)
    twos = (count - 1) // 2
    donor, sink = tallies[1:1 + 2 * twos:2], tallies[2:2 + 2 * twos:2]
    slack = jnp.minimum(donor - 1, most - sink)
    passed = jax.random.randint(jax.random.fold_in(key, 1), (twos,), 0, 1 << 20) % (slack + 1)
    tallies = tallies.at[1:1 + 2 * twos:2].set(donor - passed).at[2:2 + 2 * twos:2].set(sink + passed)
    return tallies[jax.random.permutation(jax.random.fold_in(key, 2), count)]


def noise(own_key, dims, deviation, limit, shards=(), held_as=jnp.bfloat16):
    entries = jax.random.normal(own_key, dims, jnp.float32) * deviation
    if len(shards) > 0:
        entries = block_levels(own_key, dims, shards, -0.22, 0.18) * entries
    return jnp.clip(entries, min=-limit, max=limit).astype(held_as)


def setup_inputs(seed: int = 0) -> dict:
    seeds = jax.random.split(jax.random.key(seed), 5)
    return {
        "tokens": noise(seeds[0], (TOKENS, D), 1.0, 6.0, ((0, 16), (1, 2))),
        "w_qkv": noise(seeds[1], (3, D, D), D ** -0.5, 0.125, ((1, 16), (2, 2))),
        "out_gain": jnp.clip(1.0 + 0.15 * jax.random.normal(seeds[2], (D,), jnp.float32), 0.25, 1.75),
        "seg_ids": jnp.searchsorted(jnp.cumsum(ragged_sizes(seeds[3], SEGS, TOKENS, SPAN, 2)), jnp.arange(TOKENS), side="right").astype(jnp.int32),
    }


def feature_map(values):
    return (jax.nn.elu(values.astype(jnp.float32)) + 1.0).astype(jnp.bfloat16)

def combine(earlier, later):
    first_state, first_tail = earlier
    later_state, later_tail = later
    linked = (first_tail == later_tail) | (later_tail < 0.0)
    return (later_state + jnp.where(linked, first_state, 0.0), jnp.where(later_tail < 0.0, first_tail, later_tail))

def prepare(projected, segment):
    row_count = segment.shape[0]
    head_count = projected.shape[2] // HEAD_DIM
    queries = feature_map(projected[0]).reshape(row_count, head_count, HEAD_DIM)
    key_map = feature_map(projected[1]).reshape(row_count, head_count, HEAD_DIM)
    values = projected[2].reshape(row_count, head_count, HEAD_DIM)
    seg_float = segment.astype(jnp.float32)
    tail_id = seg_float[-1]
    key_tail = jnp.where((seg_float == tail_id)[:, None, None], key_map, jnp.zeros_like(key_map))
    kv_state = jnp.einsum('thd,the->hde', key_tail.astype(jnp.float32), values.astype(jnp.float32))
    return (queries, key_map, values, seg_float, kv_state, tail_id)

def complete(queries, key_map, values, seg_float, state_in, tail_in, out_gain):
    row_count, head_count = (queries.shape[0], queries.shape[1])
    state_low = state_in.astype(jnp.bfloat16)
    prefix = jnp.einsum('thd,hde->the', queries.astype(jnp.float32), state_low.astype(jnp.float32))
    prefix = jnp.where((seg_float == tail_in)[:, None, None], prefix, 0.0)
    block_rows = min(512, row_count)
    positions = jnp.arange(row_count, dtype=jnp.int32)

    def one_block(blk_no):
        first_row = (blk_no * block_rows).astype(jnp.int32)
        query_blk = lax.dynamic_slice_in_dim(queries, first_row, block_rows, 0)
        query_pos = first_row + jnp.arange(block_rows, dtype=jnp.int32)
        query_seg = lax.dynamic_slice_in_dim(seg_float, first_row, block_rows, 0)
        scores = jnp.einsum('bhd,shd->hbs', query_blk.astype(jnp.float32), key_map.astype(jnp.float32))
        visible = (positions[None, :] <= query_pos[:, None]) & (seg_float[None, :] == query_seg[:, None])
        weights = jnp.where(visible[None], scores, 0.0).astype(jnp.bfloat16)
        return jnp.einsum('hbs,she->bhe', weights.astype(jnp.float32), values.astype(jnp.float32))
    local_part = lax.map(one_block, jnp.arange(row_count // block_rows, dtype=jnp.int32))
    numerator = local_part.reshape(row_count, head_count, HEAD_DIM) + prefix
    inv_norm = lax.rsqrt(lax.optimization_barrier(jnp.mean(numerator * numerator, axis=-1, keepdims=True)) + 1e-05)
    result = numerator * inv_norm * out_gain.reshape(head_count, HEAD_DIM)
    return result.astype(jnp.bfloat16).reshape(row_count, head_count * HEAD_DIM)

def reference(tokens, w_qkv, out_gain, seg_ids):
    blocks = tokens.reshape(N_CTX, TOK_DEV, D)
    segments = seg_ids.reshape(N_CTX, TOK_DEV)
    weights_wide = w_qkv.astype(jnp.float32)

    def one_step(carried, item):
        block_tok, segment = item
        projected = jnp.einsum('td,gde->gte', block_tok.astype(jnp.float32), weights_wide).astype(jnp.bfloat16)
        queries, key_map, values, seg_float, kv_state, tail_id = prepare(projected, segment)
        result = complete(queries, key_map, values, seg_float, carried[0], carried[1], out_gain)
        return (combine(carried, (kv_state, tail_id)), result)
    initial = (jnp.zeros((HEADS, HEAD_DIM, HEAD_DIM), jnp.float32), jnp.array(-1.0, jnp.float32))
    _, results = lax.scan(one_step, initial, (blocks, segments))
    return results.reshape(TOKENS, D)
```

```python
import functools

import jax
import jax.numpy as jnp
from jax import lax
from jax.experimental import pallas as pl
from jax.experimental.pallas import tpu as pltpu
from jax.sharding import PartitionSpec as P

HEAD_DIM = 128
CHUNK = 256
MESH = pl.DeviceIdType.MESH
F32, BF16 = jnp.float32, jnp.bfloat16
GROUPS = ((1, 0), (2, 0), (1, 1), (2, 1), (0, 0), (0, 1))


def dot(left, right, dims=((1,), (0,))):
    return lax.dot_general(left, right, (dims, ((), ())), preferred_element_type=F32)


def kernel(
    n, nh, tok_ref, w_ref, gain_ref, row_ref, col_ref, out_ref,
    wbuf, tok, qkv, local, incoming, state_out, state_got, tail_out, tail_got,
    z_send, z_recv, f_send, f_recv, s_send, s_recv,
    tok_send, tok_recv, tok_own, st_send, st_recv, tl_send, tl_recv,
):
    lines = n // 4
    span = n // 4
    rows, width = tok_ref.shape[0], tok_ref.shape[1]
    cols = wbuf.shape[-1]
    depth = n * wbuf.shape[-2]
    heads = cols // HEAD_DIM
    chunks = rows // CHUNK
    ctx, head = lax.axis_index("ctx"), lax.axis_index("head")
    a, b, c = ctx // 4, (ctx // 2) % 2, ctx % 2

    def place(a_, b_, c_):
        return (a_ * 4 + b_ * 2 + c_, head)

    def line_at(step):
        return lax.rem(a - step + lines, lines)

    def flip(flag, yes):
        return 1 - flag if yes else flag

    for g, (which, half) in enumerate(GROUPS):
        wbuf[g, a, b, c] = w_ref[which, :, half * cols:(half + 1) * cols]
    own_tail = jnp.max(row_ref[...], axis=1, keepdims=True)
    tail_out[...] = jnp.broadcast_to(own_tail, tail_out.shape)

    barrier = pltpu.get_barrier_semaphore()

    def greet(where):
        pl.semaphore_signal(barrier, inc=1, device_id=where, device_id_type=MESH)

    greet(place(a, b, 1 - c))
    greet(place(a, 1 - b, c))

    @pl.loop(1, lines)
    def _(d):
        greet(place(lax.rem(a + d, lines), b, c))

    @pl.loop(1, span + 1)
    def _(d):
        greet((lax.rem(ctx + d, n), head))
        greet((lax.rem(ctx - d + n, n), head))

    @pl.loop(1, nh)
    def _(d):
        greet((ctx, lax.rem(head + d, nh)))

    pl.semaphore_wait(barrier, 2 + (lines - 1) + 2 * span + (nh - 1))

    def remote(src, dst, send, recv, where):
        return pltpu.make_async_remote_copy(
            src_ref=src, dst_ref=dst, send_sem=send, recv_sem=recv,
            device_id=where, device_id_type=MESH,
        )

    def z_copy(g, d, slot_line, to_line):
        slot = wbuf.at[g, slot_line, b, c]
        return remote(slot, slot, z_send.at[g, d - 1], z_recv.at[g, d - 1], place(to_line, b, c))

    def f_copy(g, k, got):
        odd = g % 2
        slot = wbuf.at[g, line_at(k), flip(b, got and odd), flip(c, got and not odd)]
        where = place(a, flip(b, odd), flip(c, not odd))
        return remote(slot, slot, f_send.at[g, k], f_recv.at[g, k], where)

    def s_copy(g, k, far, got):
        odd = g % 2
        b_, c_ = (flip(b, far), flip(c, got)) if odd else (flip(b, got), flip(c, far))
        slot = wbuf.at[g, line_at(k), b_, c_]
        where = place(a, flip(b, not odd), flip(c, odd))
        at = k + (lines if far else 0)
        return remote(slot, slot, s_send.at[g, at], s_recv.at[g, at], where)

    def tok_copy(d, from_head, to_head):
        there = tok.at[:, pl.ds(pl.multiple_of(from_head * width, 128), width)]
        return remote(tok_ref, there, tok_send.at[d - 1], tok_recv.at[d - 1], (ctx, to_head))

    def state_copy(half, j):
        part = pl.ds(half * heads, heads)
        return remote(
            state_out.at[part], state_got.at[j, part], st_send.at[half, j], st_recv.at[half, j],
            (lax.rem(ctx + j + 1, n), head),
        )

    def tail_copy(j):
        return remote(
            tail_out, tail_got.at[j], tl_send.at[j], tl_recv.at[j], (lax.rem(ctx + j + 1, n), head)
        )

    def begin(pair):
        for g in pair:
            f_copy(g, 0, False).start()
            s_copy(g, 0, False, False).start()

        @pl.loop(1, lines)
        def _(d):
            for g in pair:
                z_copy(g, d, a, lax.rem(a + d, lines)).start()

    def pass_lines(pair):
        @pl.loop(1, lines)
        def _(d):
            for g in pair:
                z_copy(g, d, line_at(d), a).wait_recv()
                f_copy(g, d, False).start()
                s_copy(g, d, False, False).start()

    def pass_first(pair):
        @pl.loop(0, lines)
        def _(d):
            for g in pair:
                f_copy(g, d, True).wait_recv()
                s_copy(g, d, True, False).start()

    def finish(g):
        @pl.loop(0, lines)
        def _(d):
            s_copy(g, d, False, True).wait_recv()
            s_copy(g, d, True, True).wait_recv()

    def project(g):
        which, half = GROUPS[g]

        @pl.loop(0, chunks)
        def _(i):
            part = pl.ds(pl.multiple_of(i * CHUNK, CHUNK), CHUNK)
            weights = wbuf[g].reshape(depth, cols)
            got = dot(tok[part, :], weights).astype(BF16)
            if which < 2:
                wide = got.astype(F32)
                got = jnp.where(wide > 0.0, wide + 1.0, jnp.exp(jnp.minimum(wide, 0.0))).astype(BF16)
            qkv[which, part, half * cols:(half + 1) * cols] = got

    def own_states(half):
        for h in range(heads):
            at = half * heads + h
            lanes = pl.ds(at * HEAD_DIM, HEAD_DIM)
            state = jnp.zeros((HEAD_DIM, HEAD_DIM), F32)
            before = None
            for i in range(chunks):
                part = pl.ds(i * CHUNK, CHUNK)
                ids = row_ref[:, part]
                first = jnp.min(ids, axis=1, keepdims=True)
                tail = jnp.max(ids, axis=1, keepdims=True)
                if i > 0:
                    state = jnp.where(before == first, state, 0.0)
                local[i, at] = state
                keys = qkv[1, part, lanes]
                keys = jnp.where(col_ref[part, :] == tail, keys, jnp.zeros_like(keys))
                fresh = dot(keys, qkv[2, part, lanes], ((0,), (0,)))
                state = jnp.where(first == tail, state, 0.0) + fresh
                before = tail
            state_out[at] = state.astype(BF16)

        @pl.loop(0, span)
        def _(j):
            state_copy(half, j).start()

    def add_states():
        first = jnp.min(row_ref[:, pl.ds(0, CHUNK)], axis=1, keepdims=True)
        incoming[...] = jnp.zeros_like(incoming)

        @pl.loop(0, span)
        def _(j):
            tail_copy(j).wait_recv()
            for half in range(2):
                state_copy(half, j).wait_recv()
            ids = tail_got[j][0:1, :] + jnp.where(ctx > j, 0, -1000)
            linked = ids == first
            for at in range(2 * heads):
                incoming[at] += jnp.where(linked, state_got[j, at].astype(F32), 0.0)

        for i in range(chunks):
            ids = row_ref[:, pl.ds(i * CHUNK, CHUNK)]
            here = jnp.min(ids, axis=1, keepdims=True)
            for at in range(2 * heads):
                local[i, at] += jnp.where(here == first, incoming[at], 0.0)

    def attend(half):
        @pl.loop(0, chunks)
        def _(i):
            part = pl.ds(pl.multiple_of(i * CHUNK, CHUNK), CHUNK)
            ids_row, ids_col = row_ref[:, part], col_ref[part, :]
            first = jnp.min(ids_row, axis=1, keepdims=True)
            later = lax.broadcasted_iota(jnp.int32, (CHUNK, CHUNK), 0)
            sooner = lax.broadcasted_iota(jnp.int32, (CHUNK, CHUNK), 1)
            visible = (sooner <= later) & (ids_row == ids_col)
            reached = ids_col == first
            for h in range(heads):
                at = half * heads + h
                lanes = pl.ds(at * HEAD_DIM, HEAD_DIM)
                query = qkv[0, part, lanes]
                scores = dot(query, qkv[1, part, lanes], ((1,), (1,)))
                scores = jnp.where(visible, scores, 0.0).astype(BF16)
                total = dot(scores, qkv[2, part, lanes])
                prefix = dot(query, local[i, at].astype(BF16))
                total = total + jnp.where(reached, prefix, 0.0)
                scale = lax.rsqrt(jnp.mean(total * total, axis=1, keepdims=True) + 1e-05)
                out_ref[part, lanes] = (total * scale * gain_ref[:, lanes]).astype(BF16)

    pairs = ((0, 1), (2, 3), (4, 5))
    begin(pairs[0])

    @pl.loop(1, nh)
    def _(d):
        tok_copy(d, head, lax.rem(head + d, nh)).start()

    own = pltpu.make_async_copy(
        tok_ref, tok.at[:, pl.ds(pl.multiple_of(head * width, 128), width)], tok_own
    )
    own.start()

    @pl.loop(0, span)
    def _(j):
        tail_copy(j).start()

    begin(pairs[1])
    pass_lines(pairs[0])
    pass_first(pairs[0])
    own.wait()

    @pl.loop(1, nh)
    def _(d):
        tok_copy(d, lax.rem(head - d + nh, nh), head).wait_recv()

    pass_lines(pairs[1])
    for g in pairs[0]:
        finish(g)
        project(g)
    begin(pairs[2])
    own_states(0)
    pass_first(pairs[1])
    pass_lines(pairs[2])
    for g in pairs[1]:
        finish(g)
        project(g)
    own_states(1)
    pass_first(pairs[2])
    add_states()
    for g in pairs[2]:
        finish(g)
        project(g)
        attend(GROUPS[g][1])

    @pl.loop(1, lines)
    def _(d):
        for g in range(len(GROUPS)):
            z_copy(g, d, a, lax.rem(a + d, lines)).wait_send()

    @pl.loop(0, lines)
    def _(d):
        for g in range(len(GROUPS)):
            f_copy(g, d, False).wait_send()
            s_copy(g, d, False, False).wait_send()
            s_copy(g, d, True, False).wait_send()

    @pl.loop(1, nh)
    def _(d):
        tok_copy(d, head, lax.rem(head + d, nh)).wait_send()

    @pl.loop(0, span)
    def _(j):
        tail_copy(j).wait_send()
        for half in range(2):
            state_copy(half, j).wait_send()


def per_device(n, nh, tokens, w_qkv, out_gain, seg_ids):
    rows, width = tokens.shape
    part_rows, own_cols = w_qkv.shape[1:]
    cols = own_cols // 2
    heads = own_cols // HEAD_DIM
    lines = span = n // 4
    groups = len(GROUPS)
    vmem = pl.BlockSpec(memory_space=pltpu.VMEM)
    dma = pltpu.SemaphoreType.DMA
    state = (heads, HEAD_DIM, HEAD_DIM)
    return pl.pallas_call(
        functools.partial(kernel, n, nh),
        out_shape=jax.ShapeDtypeStruct((rows, own_cols), BF16),
        in_specs=[pl.BlockSpec(memory_space=pl.ANY), vmem, vmem, vmem, vmem],
        out_specs=vmem,
        scratch_shapes=[
            pltpu.VMEM((groups, lines, 2, 2, part_rows, cols), BF16),
            pltpu.VMEM((rows, width * nh), BF16),
            pltpu.VMEM((3, rows, own_cols), BF16),
            pltpu.VMEM((rows // CHUNK,) + state, F32),
            pltpu.VMEM(state, F32),
            pltpu.VMEM(state, BF16),
            pltpu.VMEM((span,) + state, BF16),
            pltpu.VMEM((8, HEAD_DIM), jnp.int32),
            pltpu.VMEM((span, 8, HEAD_DIM), jnp.int32),
            dma((groups, lines - 1)), dma((groups, lines - 1)),
            dma((groups, lines)), dma((groups, lines)),
            dma((groups, 2 * lines)), dma((groups, 2 * lines)),
            dma((nh - 1,)), dma((nh - 1,)), dma,
            dma((2, span)), dma((2, span)),
            dma((span,)), dma((span,)),
        ],
        compiler_params=pltpu.CompilerParams(
            collective_id=0, has_side_effects=True, vmem_limit_bytes=56 * 1024 * 1024
        ),
        cost_estimate=pl.CostEstimate(
            flops=2 * rows * width * nh * own_cols * 3,
            bytes_accessed=4 * rows * width, transcendentals=rows * own_cols,
        ),
    )(
        tokens, w_qkv, out_gain.reshape(1, own_cols),
        seg_ids.reshape(1, rows), seg_ids.reshape(rows, 1),
    )


def solution(mesh):
    placed = (P("ctx", "head"), P(None, "ctx", "head"), P("head"), P("ctx"))
    sizes = (mesh.shape["ctx"], mesh.shape["head"])
    return jax.shard_map(
        functools.partial(per_device, *sizes),
        mesh=mesh, in_specs=placed, out_specs=P("ctx", "head"), check_vma=False,
    )
```

```python
import functools

import jax
import jax.numpy as jnp
from jax import lax
from jax.experimental import pallas as pl
from jax.experimental.pallas import tpu as pltpu
from jax.sharding import PartitionSpec as P

HEAD_DIM = 128
CHUNK = 256
MESH = pl.DeviceIdType.MESH
F32, BF16 = jnp.float32, jnp.bfloat16


def groups_of(halves):
    keys_values = tuple((which, half) for half in range(halves) for which in (1, 2))
    return keys_values + tuple((0, half) for half in range(halves))


def dot(left, right, dims=((1,), (0,))):
    return lax.dot_general(left, right, (dims, ((), ())), preferred_element_type=F32)


def kernel(
    n, nh, halves, tok_ref, w_ref, gain_ref, row_ref, out_ref,
    wbuf, wout, tok, qkv, outs, local, incoming, state_out, state_got, row, col, tail_out, tail_got,
    x_send, x_recv, z_send, z_recv, y_send, y_recv,
    tok_send, tok_recv, tok_own, px_send, px_recv, ph_send, ph_recv,
    st_send, st_recv, tl_send, tl_recv, row_send, row_recv, out_send, out_recv, out_own,
):
    lines = n // 4
    pairs = n // 2
    span = n // 8
    rows, width = tok_ref.shape[0], tok_ref.shape[1]
    cols = wbuf.shape[-1]
    depth = n * wbuf.shape[-2]
    heads = cols // HEAD_DIM
    chunks = rows // CHUNK
    groups = groups_of(halves)
    last = len(groups) - 1
    ctx, head = lax.axis_index("ctx"), lax.axis_index("head")
    a, b, c = ctx // 4, (ctx // 2) % 2, ctx % 2
    pair = ctx // 2

    def place(a_, b_, c_):
        return (a_ * 4 + b_ * 2 + c_, head)

    def line_at(step):
        return lax.rem(a - step + lines, lines)

    for g, (which, half) in enumerate(groups):
        keep = pl.ds(pl.multiple_of((c * halves + half) * cols, 128), cols)
        give = pl.ds(pl.multiple_of(((1 - c) * halves + half) * cols, 128), cols)
        wbuf[g, a, b, c] = w_ref[which, :, keep]
        wout[g] = w_ref[which, :, give]
    row[c] = row_ref[...]

    barrier = pltpu.get_barrier_semaphore()

    def greet(where):
        pl.semaphore_signal(barrier, inc=1, device_id=where, device_id_type=MESH)

    greet(place(a, b, 1 - c))
    greet(place(a, 1 - b, c))

    @pl.loop(1, lines)
    def _(d):
        greet(place(lax.rem(a + d, lines), b, c))

    @pl.loop(1, span + 1)
    def _(d):
        greet((lax.rem(pair + d, pairs) * 2 + c, head))
        greet((lax.rem(pair - d + pairs, pairs) * 2 + c, head))

    @pl.loop(1, nh)
    def _(d):
        greet((ctx, lax.rem(head + d, nh)))

    pl.semaphore_wait(barrier, 2 + (lines - 1) + 2 * span + (nh - 1))

    def remote(src, dst, send, recv, where):
        return pltpu.make_async_remote_copy(
            src_ref=src, dst_ref=dst, send_sem=send, recv_sem=recv,
            device_id=where, device_id_type=MESH,
        )

    def x_copy(g, c_):
        return remote(
            wout.at[g], wbuf.at[g, a, b, c_], x_send.at[g], x_recv.at[g], place(a, b, 1 - c)
        )

    def z_copy(g, d, far, slot_line, to_line):
        slot = wbuf.at[g, slot_line, b, 1 - c if far else c]
        at = d - 1 + (lines - 1 if far else 0)
        return remote(slot, slot, z_send.at[g, at], z_recv.at[g, at], place(to_line, b, c))

    def y_copy(g, k, far, b_):
        slot = wbuf.at[g, line_at(k), b_, 1 - c if far else c]
        at = k + (lines if far else 0)
        return remote(slot, slot, y_send.at[g, at], y_recv.at[g, at], place(a, 1 - b, c))

    def features(of):
        return pl.ds(pl.multiple_of(of * width, 128), width)

    def own_rows(of):
        return pl.ds(pl.multiple_of(of * rows, CHUNK), rows)

    def piece(of, i):
        return pl.ds(pl.multiple_of(of * rows + i * CHUNK, CHUNK), CHUNK)

    def tok_copy(d, of, to):
        there = tok.at[own_rows(c), features(of)]
        return remote(tok_ref, there, tok_send.at[d - 1], tok_recv.at[d - 1], (ctx, to))

    def px_copy(i, of):
        return remote(
            tok_ref.at[pl.ds(i * CHUNK, CHUNK)], tok.at[piece(of, i), features(head)],
            px_send.at[i], px_recv.at[i], place(a, b, 1 - c),
        )

    def ph_copy(i, d, of, to):
        there = tok.at[piece(1 - c, i), features(of)]
        return remote(there, there, ph_send.at[i, d - 1], ph_recv.at[i, d - 1], (ctx, to))

    def state_copy(half, j):
        part = pl.ds(half * heads, heads)
        return remote(
            state_out.at[part], state_got.at[j, part], st_send.at[half, j], st_recv.at[half, j],
            (lax.rem(pair + j + 1, pairs) * 2 + c, head),
        )

    def tail_copy(j):
        return remote(
            tail_out, tail_got.at[j], tl_send.at[j], tl_recv.at[j],
            (lax.rem(pair + j + 1, pairs) * 2 + c, head),
        )

    def row_copy(c_):
        return remote(row.at[c_], row.at[c_], row_send, row_recv, place(a, b, 1 - c))

    def out_copy(half, i, of):
        part = pl.ds(half * cols, cols)
        there = pl.ds(pl.multiple_of((of * halves + half) * cols, 128), cols)
        at = pl.ds(pl.multiple_of(i * CHUNK, CHUNK), CHUNK)
        return remote(
            outs.at[piece(1 - c, i), part], out_ref.at[at, there],
            out_send.at[half, i], out_recv.at[half, i], place(a, b, 1 - c),
        )

    def out_keep(half):
        there = pl.ds(pl.multiple_of((c * halves + half) * cols, 128), cols)
        return pltpu.make_async_copy(
            outs.at[own_rows(c), pl.ds(half * cols, cols)], out_ref.at[:, there], out_own.at[half]
        )

    def next_head(d):
        return lax.rem(head + d, nh)

    def prior_head(d):
        return lax.rem(head - d + nh, nh)

    def spread(g, far):
        y_copy(g, 0, far, b).start()

        @pl.loop(1, lines)
        def _(d):
            z_copy(g, d, far, a, lax.rem(a + d, lines)).start()

    def begin(g):
        x_copy(g, c).start()
        spread(g, False)

    def pass_partner(g):
        x_copy(g, 1 - c).wait_recv()
        spread(g, True)

    def pass_lines(g):
        @pl.loop(1, lines)
        def _(d):
            for far in (False, True):
                z_copy(g, d, far, line_at(d), a).wait_recv()
                y_copy(g, d, far, b).start()

    def finish(g):
        @pl.loop(0, lines)
        def _(d):
            for far in (False, True):
                y_copy(g, d, far, 1 - b).wait_recv()

    def project(g, of, i, height):
        which, half = groups[g]
        part = pl.ds(pl.multiple_of(of * rows + i * height, height), height)
        got = dot(tok[part, :], wbuf[g].reshape(depth, cols)).astype(BF16)
        if which < 2:
            wide = got.astype(F32)
            got = jnp.where(wide > 0.0, wide + 1.0, jnp.exp(jnp.minimum(wide, 0.0))).astype(BF16)
        qkv[which, part, half * cols:(half + 1) * cols] = got

    def project_own(g):
        @pl.loop(0, rows // 512)
        def _(i):
            project(g, c, i, 512)

    def ids_of(i):
        return row[i // chunks, :, (i % chunks) * CHUNK:(i % chunks + 1) * CHUNK]

    def least(ids):
        return jnp.min(ids, axis=1, keepdims=True)

    def most(ids):
        return jnp.max(ids, axis=1, keepdims=True)

    def own_states(half):
        for h in range(heads):
            at = half * heads + h
            lanes = pl.ds(at * HEAD_DIM, HEAD_DIM)
            state = jnp.zeros((HEAD_DIM, HEAD_DIM), F32)
            before = None
            for i in range(2 * chunks):
                part = pl.ds(i * CHUNK, CHUNK)
                first, tail = least(ids_of(i)), most(ids_of(i))
                if i > 0:
                    state = jnp.where(before == first, state, 0.0)
                local[i, at] = state
                keys = qkv[1, part, lanes]
                keys = jnp.where(col[part, 0:1] == tail, keys, jnp.zeros_like(keys))
                fresh = dot(keys, qkv[2, part, lanes], ((0,), (0,)))
                state = jnp.where(first == tail, state, 0.0) + fresh
                before = tail
            state_out[at] = state.astype(BF16)

        @pl.loop(0, span)
        def _(j):
            state_copy(half, j).start()

    def add_states():
        first = least(ids_of(0))
        incoming[...] = jnp.zeros_like(incoming)

        @pl.loop(0, span)
        def _(j):
            tail_copy(j).wait_recv()
            for half in range(halves):
                state_copy(half, j).wait_recv()
            ids = tail_got[j][0:1, :] + jnp.where(pair > j, 0, -1000)
            linked = ids == first
            for at in range(halves * heads):
                incoming[at] += jnp.where(linked, state_got[j, at].astype(F32), 0.0)

        for i in range(2 * chunks):
            here = least(ids_of(i))
            for at in range(halves * heads):
                local[i, at] += jnp.where(here == first, incoming[at], 0.0)

    def attend(half, of, i):
        part = piece(of, i)
        ids_row = row[of, :, pl.ds(pl.multiple_of(i * CHUNK, CHUNK), CHUNK)]
        ids_col = col[part, 0:1]
        later = lax.broadcasted_iota(jnp.int32, (CHUNK, CHUNK), 0)
        sooner = lax.broadcasted_iota(jnp.int32, (CHUNK, CHUNK), 1)
        visible = (sooner <= later) & (ids_row == ids_col)
        reached = ids_col == least(ids_row)
        for h in range(heads):
            at = half * heads + h
            lanes = pl.ds(at * HEAD_DIM, HEAD_DIM)
            query = qkv[0, part, lanes]
            scores = dot(query, qkv[1, part, lanes], ((1,), (1,)))
            scores = jnp.where(visible, scores, 0.0).astype(BF16)
            total = dot(scores, qkv[2, part, lanes])
            prefix = dot(query, local[of * chunks + i, at].astype(BF16))
            total = total + jnp.where(reached, prefix, 0.0)
            scale = lax.rsqrt(jnp.mean(total * total, axis=1, keepdims=True) + 1e-05)
            gain = gain_ref[:, pl.ds(pl.multiple_of((c * halves * heads + at) * HEAD_DIM, 128), HEAD_DIM)]
            outs[part, lanes] = (total * scale * gain).astype(BF16)

    def attend_all(half):
        @pl.loop(0, chunks)
        def _(i):
            attend(half, 1 - c, i)
            out_copy(half, i, c).start()

        @pl.loop(0, chunks)
        def _(i):
            attend(half, c, i)

        out_keep(half).start()

    begin(0)
    row_copy(c).start()

    @pl.loop(1, nh)
    def _(d):
        tok_copy(d, head, next_head(d)).start()

    own = pltpu.make_async_copy(tok_ref, tok.at[own_rows(c), features(head)], tok_own)
    own.start()
    begin(1)
    begin(2)
    px_copy(0, c).start()
    pass_partner(0)
    pass_partner(1)
    row_copy(1 - c).wait_recv()
    tail_out[...] = jnp.broadcast_to(most(row[1]), tail_out.shape)

    @pl.loop(0, span)
    def _(j):
        tail_copy(j).start()

    for i in range(2 * chunks):
        col[pl.ds(i * CHUNK, CHUNK), :] = jnp.broadcast_to(ids_of(i), (HEAD_DIM, CHUNK)).T
    pass_lines(0)

    for g in range(last + 1):
        if g + 3 <= last:
            begin(g + 3)
        if g <= last - 2:
            for i in range(g + 1, chunks if g == last - 2 else min(g + 2, chunks)):
                px_copy(i, c).start()
        if g + 2 <= last:
            pass_partner(g + 2)
        if g + 1 <= last:
            pass_lines(g + 1)
        if g == 0:
            own.wait()

            @pl.loop(1, nh)
            def _(d):
                tok_copy(d, prior_head(d), head).wait_recv()

        if g == last:
            ready, fresh = chunks, ()
        else:
            ready = min(max(g - 1, 0), chunks)
            fresh = range(ready, chunks if g == last - 1 else min(g, chunks))
        for i in fresh:
            px_copy(i, 1 - c).wait_recv()

            @pl.loop(1, nh)
            def _(d):
                ph_copy(i, d, head, next_head(d)).start()

        finish(g)
        project_own(g)
        if ready > 0:
            @pl.loop(0, ready)
            def _(i):
                project(g, 1 - c, i, CHUNK)

        for i in fresh:
            @pl.loop(1, nh)
            def _(d):
                ph_copy(i, d, prior_head(d), head).wait_recv()

            for earlier in range(g + 1):
                project(earlier, 1 - c, i, CHUNK)
        if g == last - 1:
            for half in range(halves):
                own_states(half)
            add_states()
            for half in range(halves - 1):
                attend_all(half)
    attend_all(halves - 1)

    for g in range(last + 1):
        x_copy(g, c).wait_send()

        @pl.loop(1, lines)
        def _(d):
            for far in (False, True):
                z_copy(g, d, far, a, lax.rem(a + d, lines)).wait_send()

        @pl.loop(0, lines)
        def _(d):
            for far in (False, True):
                y_copy(g, d, far, b).wait_send()

    row_copy(c).wait_send()

    @pl.loop(1, nh)
    def _(d):
        tok_copy(d, head, next_head(d)).wait_send()

    for i in range(chunks):
        px_copy(i, c).wait_send()

        @pl.loop(1, nh)
        def _(d):
            ph_copy(i, d, head, next_head(d)).wait_send()

    @pl.loop(0, span)
    def _(j):
        tail_copy(j).wait_send()
        for half in range(halves):
            state_copy(half, j).wait_send()

    for half in range(halves):
        out_keep(half).wait()

        @pl.loop(0, chunks)
        def _(i):
            out_copy(half, i, c).wait_send()
            out_copy(half, i, 1 - c).wait_recv()


def per_device(n, nh, tokens, w_qkv, out_gain, seg_ids):
    rows, width = tokens.shape
    part_rows, own_cols = w_qkv.shape[1:]
    halves = 2 if own_cols >= 4 * HEAD_DIM else 1
    cols = own_cols // (2 * halves)
    heads = own_cols // 2 // HEAD_DIM
    lines, span, chunks = n // 4, n // 8, rows // CHUNK
    groups = 3 * halves
    vmem = pl.BlockSpec(memory_space=pltpu.VMEM)
    hbm = pl.BlockSpec(memory_space=pl.ANY)
    dma = pltpu.SemaphoreType.DMA
    state = (heads, HEAD_DIM, HEAD_DIM)
    return pl.pallas_call(
        functools.partial(kernel, n, nh, halves),
        out_shape=jax.ShapeDtypeStruct((rows, own_cols), BF16),
        in_specs=[hbm, vmem, vmem, vmem],
        out_specs=hbm,
        scratch_shapes=[
            pltpu.VMEM((groups, lines, 2, 2, part_rows, cols), BF16),
            pltpu.VMEM((groups, part_rows, cols), BF16),
            pltpu.VMEM((2 * rows, width * nh), BF16),
            pltpu.VMEM((3, 2 * rows, halves * cols), BF16),
            pltpu.VMEM((2 * rows, halves * cols), BF16),
            pltpu.VMEM((2 * chunks,) + state, F32),
            pltpu.VMEM(state, F32),
            pltpu.VMEM(state, BF16),
            pltpu.VMEM((span,) + state, BF16),
            pltpu.VMEM((2, 1, rows), jnp.int32),
            pltpu.VMEM((2 * rows, HEAD_DIM), jnp.int32),
            pltpu.VMEM((8, HEAD_DIM), jnp.int32),
            pltpu.VMEM((span, 8, HEAD_DIM), jnp.int32),
            dma((groups,)), dma((groups,)),
            dma((groups, 2 * lines - 2)), dma((groups, 2 * lines - 2)),
            dma((groups, 2 * lines)), dma((groups, 2 * lines)),
            dma((nh - 1,)), dma((nh - 1,)), dma,
            dma((chunks,)), dma((chunks,)),
            dma((chunks, nh - 1)), dma((chunks, nh - 1)),
            dma((halves, span)), dma((halves, span)),
            dma((span,)), dma((span,)),
            dma, dma,
            dma((halves, chunks)), dma((halves, chunks)), dma((halves,)),
        ],
        compiler_params=pltpu.CompilerParams(
            collective_id=0, has_side_effects=True, vmem_limit_bytes=56 * 1024 * 1024
        ),
        cost_estimate=pl.CostEstimate(
            flops=2 * rows * width * nh * own_cols * 3,
            bytes_accessed=4 * rows * width, transcendentals=rows * own_cols,
        ),
    )(tokens, w_qkv, out_gain.reshape(1, own_cols), seg_ids.reshape(1, rows))


def solution(mesh):
    placed = (P("ctx", "head"), P(None, "ctx", "head"), P("head"), P("ctx"))
    sizes = (mesh.shape["ctx"], mesh.shape["head"])
    return jax.shard_map(
        functools.partial(per_device, *sizes),
        mesh=mesh, in_specs=placed, out_specs=P("ctx", "head"), check_vma=False,
    )
```

```python
import functools

import jax
import jax.numpy as jnp
from jax import lax
from jax.experimental import pallas as pl
from jax.experimental.pallas import tpu as pltpu
from jax.sharding import PartitionSpec as P

HEAD_DIM = 128
CHUNK = 256
MESH = pl.DeviceIdType.MESH
F32, BF16 = jnp.float32, jnp.bfloat16


def groups_of(heads):
    if heads % 4:
        return ((1, 0, heads), (2, 0, heads), (0, 0, heads))
    half = heads // 2
    first = tuple((which, 0, half) for which in (1, 2, 0))
    second = tuple((which, half, half) for which in (1, 2))
    return first + second + ((0, half, half // 2), (0, half + half // 2, half // 2))


def dot(left, right, dims=((1,), (0,))):
    return lax.dot_general(left, right, (dims, ((), ())), preferred_element_type=F32)


def kernel(
    n, nh, groups, tok_ref, w_ref, gain_ref, row_ref, out_ref, wbufs, wouts, tok, qkv, outs, local, incoming, state_out, state_got, row, col, tail_out, tail_got,
    x_send, x_recv, z_send, z_recv, y_send, y_recv,
    tok_send, tok_recv, tok_own, px_send, px_recv, ph_send, ph_recv,
    st_send, st_recv, tl_send, tl_recv, row_send, row_recv, out_send, out_recv, out_own,
):
    lines = n // 4
    pairs = n // 2
    span = n // 8
    rows, width = tok_ref.shape[0], tok_ref.shape[1]
    depth = n * w_ref.shape[1]
    all_heads = w_ref.shape[2] // 2 // HEAD_DIM
    heads = groups[0][2]
    halves = all_heads // heads
    chunks = rows // CHUNK
    last = len(groups) - 1
    ctx, head = lax.axis_index("ctx"), lax.axis_index("head")
    a, b, c = ctx // 4, (ctx // 2) % 2, ctx % 2
    pair = ctx // 2

    def place(a_, b_, c_):
        return (a_ * 4 + b_ * 2 + c_, head)

    def line_at(step):
        return lax.rem(a - step + lines, lines)

    for g, (which, first, count) in enumerate(groups):
        span_of = count * HEAD_DIM
        keep = pl.ds(pl.multiple_of((c * all_heads + first) * HEAD_DIM, 128), span_of)
        give = pl.ds(pl.multiple_of(((1 - c) * all_heads + first) * HEAD_DIM, 128), span_of)
        wbufs[g][a, b, c] = w_ref[which, :, keep]
        wouts[g][...] = w_ref[which, :, give]
    row[c] = row_ref[...]

    barrier = pltpu.get_barrier_semaphore()

    def greet(where):
        pl.semaphore_signal(barrier, inc=1, device_id=where, device_id_type=MESH)

    greet(place(a, b, 1 - c))
    greet(place(a, 1 - b, c))

    @pl.loop(1, lines)
    def _(d):
        greet(place(lax.rem(a + d, lines), b, c))

    @pl.loop(1, span + 1)
    def _(d):
        greet((lax.rem(pair + d, pairs) * 2 + c, head))
        greet((lax.rem(pair - d + pairs, pairs) * 2 + c, head))

    @pl.loop(1, nh)
    def _(d):
        greet((ctx, lax.rem(head + d, nh)))

    pl.semaphore_wait(barrier, 2 + (lines - 1) + 2 * span + (nh - 1))

    def remote(src, dst, send, recv, where):
        return pltpu.make_async_remote_copy(
            src_ref=src, dst_ref=dst, send_sem=send, recv_sem=recv,
            device_id=where, device_id_type=MESH,
        )

    def x_copy(g, c_):
        return remote(
            wouts[g], wbufs[g].at[a, b, c_], x_send.at[g], x_recv.at[g], place(a, b, 1 - c)
        )

    def z_copy(g, d, far, slot_line, to_line):
        slot = wbufs[g].at[slot_line, b, 1 - c if far else c]
        at = d - 1 + (lines - 1 if far else 0)
        return remote(slot, slot, z_send.at[g, at], z_recv.at[g, at], place(to_line, b, c))

    def y_copy(g, k, far, b_):
        slot = wbufs[g].at[line_at(k), b_, 1 - c if far else c]
        at = k + (lines if far else 0)
        return remote(slot, slot, y_send.at[g, at], y_recv.at[g, at], place(a, 1 - b, c))

    def features(of):
        return pl.ds(pl.multiple_of(of * width, 128), width)

    def own_rows(of):
        return pl.ds(pl.multiple_of(of * rows, CHUNK), rows)

    def piece(of, i):
        return pl.ds(pl.multiple_of(of * rows + i * CHUNK, CHUNK), CHUNK)

    def tok_copy(d, of, to):
        there = tok.at[own_rows(c), features(of)]
        return remote(tok_ref, there, tok_send.at[d - 1], tok_recv.at[d - 1], (ctx, to))

    def px_copy(i, of):
        return remote(
            tok_ref.at[pl.ds(i * CHUNK, CHUNK)], tok.at[piece(of, i), features(head)],
            px_send.at[i], px_recv.at[i], place(a, b, 1 - c),
        )

    def ph_copy(i, d, of, to):
        there = tok.at[piece(1 - c, i), features(of)]
        return remote(there, there, ph_send.at[i, d - 1], ph_recv.at[i, d - 1], (ctx, to))

    def state_copy(half, j):
        part = pl.ds(half * heads, heads)
        return remote(
            state_out.at[part], state_got.at[j, part], st_send.at[half, j], st_recv.at[half, j],
            (lax.rem(pair + j + 1, pairs) * 2 + c, head),
        )

    def tail_copy(j):
        return remote(
            tail_out, tail_got.at[j], tl_send.at[j], tl_recv.at[j],
            (lax.rem(pair + j + 1, pairs) * 2 + c, head),
        )

    def row_copy(c_):
        return remote(row.at[c_], row.at[c_], row_send, row_recv, place(a, b, 1 - c))

    def lanes_of(g):
        return pl.ds(groups[g][1] * HEAD_DIM, groups[g][2] * HEAD_DIM)

    def out_lanes(g, of):
        start = pl.multiple_of((of * all_heads + groups[g][1]) * HEAD_DIM, 128)
        return pl.ds(start, groups[g][2] * HEAD_DIM)

    def out_copy(g, i, of):
        at = pl.ds(pl.multiple_of(i * CHUNK, CHUNK), CHUNK)
        return remote(
            outs.at[piece(1 - c, i), lanes_of(g)], out_ref.at[at, out_lanes(g, of)],
            out_send.at[g, i], out_recv.at[g, i], place(a, b, 1 - c),
        )

    def out_keep(g):
        return pltpu.make_async_copy(
            outs.at[own_rows(c), lanes_of(g)], out_ref.at[:, out_lanes(g, c)], out_own.at[g]
        )

    def next_head(d):
        return lax.rem(head + d, nh)

    def prior_head(d):
        return lax.rem(head - d + nh, nh)

    def spread(g, far):
        y_copy(g, 0, far, b).start()

        @pl.loop(1, lines)
        def _(d):
            z_copy(g, d, far, a, lax.rem(a + d, lines)).start()

    def begin(g):
        if g <= last:
            x_copy(g, c).start()

    def own_part(g):
        if g <= last:
            spread(g, False)

    def pass_partner(g):
        if g <= last:
            x_copy(g, 1 - c).wait_recv()
            spread(g, True)

    def pass_lines(g):
        for far in (False, True):
            @pl.loop(1, lines if g <= last else 1)
            def _(d):
                z_copy(g, d, far, line_at(d), a).wait_recv()
                y_copy(g, d, far, b).start()

    def finish(g):
        @pl.loop(0, lines)
        def _(d):
            for far in (False, True):
                y_copy(g, d, far, 1 - b).wait_recv()

    def project(g, of, i, height):
        which = groups[g][0]
        part = pl.ds(pl.multiple_of(of * rows + i * height, height), height)
        got = dot(tok[part, :], wbufs[g][...].reshape(depth, groups[g][2] * HEAD_DIM)).astype(BF16)
        if which < 2:
            wide = got.astype(F32)
            got = jnp.where(wide > 0.0, wide + 1.0, jnp.exp(jnp.minimum(wide, 0.0))).astype(BF16)
        qkv[which, part, lanes_of(g)] = got

    def project_own(g):
        @pl.loop(0, rows // 512)
        def _(i):
            project(g, c, i, 512)

    def ids_of(i):
        return row[i // chunks, :, (i % chunks) * CHUNK:(i % chunks + 1) * CHUNK]

    def least(ids):
        return jnp.min(ids, axis=1, keepdims=True)

    def most(ids):
        return jnp.max(ids, axis=1, keepdims=True)

    def own_states(half):
        for h in range(heads):
            at = half * heads + h
            lanes = pl.ds(at * HEAD_DIM, HEAD_DIM)
            state = jnp.zeros((HEAD_DIM, HEAD_DIM), F32)
            before = None
            for i in range(2 * chunks):
                part = pl.ds(i * CHUNK, CHUNK)
                first, tail = least(ids_of(i)), most(ids_of(i))
                if i > 0:
                    state = jnp.where(before == first, state, 0.0)
                local[i, at] = state
                keys = qkv[1, part, lanes]
                keys = jnp.where(col[part, 0:1] == tail, keys, jnp.zeros_like(keys))
                fresh = dot(keys, qkv[2, part, lanes], ((0,), (0,)))
                state = jnp.where(first == tail, state, 0.0) + fresh
                before = tail
            state_out[at] = state.astype(BF16)

        @pl.loop(0, span)
        def _(j):
            state_copy(half, j).start()

    def add_states(half):
        first = least(ids_of(0))
        own = range(half * heads, (half + 1) * heads)
        for at in own:
            incoming[at] = jnp.zeros((HEAD_DIM, HEAD_DIM), F32)

        @pl.loop(0, span)
        def _(j):
            if half == 0:
                tail_copy(j).wait_recv()
            state_copy(half, j).wait_recv()
            ids = tail_got[j][0:1, :] + jnp.where(pair > j, 0, -1000)
            linked = ids == first
            for at in own:
                incoming[at] += jnp.where(linked, state_got[j, at].astype(F32), 0.0)

        for i in range(2 * chunks):
            here = least(ids_of(i))
            for at in own:
                local[i, at] += jnp.where(here == first, incoming[at], 0.0)

    def attend(g, of, i):
        part = piece(of, i)
        ids_row = row[of, :, pl.ds(pl.multiple_of(i * CHUNK, CHUNK), CHUNK)]
        ids_col = col[part, 0:1]
        later = lax.broadcasted_iota(jnp.int32, (CHUNK, CHUNK), 0)
        sooner = lax.broadcasted_iota(jnp.int32, (CHUNK, CHUNK), 1)
        visible = (sooner <= later) & (ids_row == ids_col)
        reached = ids_col == least(ids_row)
        for at in range(groups[g][1], groups[g][1] + groups[g][2]):
            lanes = pl.ds(at * HEAD_DIM, HEAD_DIM)
            query = qkv[0, part, lanes]
            scores = dot(query, qkv[1, part, lanes], ((1,), (1,)))
            scores = jnp.where(visible, scores, 0.0).astype(BF16)
            total = dot(scores, qkv[2, part, lanes])
            prefix = dot(query, local[of * chunks + i, at].astype(BF16))
            total = total + jnp.where(reached, prefix, 0.0)
            scale = lax.rsqrt(jnp.mean(total * total, axis=1, keepdims=True) + 1e-05)
            gain = gain_ref[:, pl.ds(pl.multiple_of((c * all_heads + at) * HEAD_DIM, 128), HEAD_DIM)]
            outs[part, lanes] = (total * scale * gain).astype(BF16)

    def attend_partner(g, fresh):
        @pl.loop(0, rows // 512)
        def _(i):
            if fresh:
                project(g, 1 - c, i, 512)
            for part in range(512 // CHUNK):
                attend(g, 1 - c, i * (512 // CHUNK) + part)
            for part in range(512 // CHUNK):
                out_copy(g, i * (512 // CHUNK) + part, c).start()

    def attend_own(g, fresh):
        @pl.loop(0, rows // 512)
        def _(i):
            if fresh:
                project(g, c, i, 512)
            for part in range(512 // CHUNK):
                attend(g, c, i * (512 // CHUNK) + part)

        out_keep(g).start()

    def pass_piece(i):
        px_copy(i, 1 - c).wait_recv()

        @pl.loop(1, nh)
        def _(d):
            ph_copy(i, d, head, next_head(d)).start()

    def use_piece(i, of_groups):
        @pl.loop(1, nh)
        def _(d):
            ph_copy(i, d, prior_head(d), head).wait_recv()

        for g in of_groups:
            project(g, 1 - c, i, CHUNK)

    def project_pieces(g, count):
        @pl.loop(0, count)
        def _(i):
            project(g, 1 - c, i, CHUNK)

    def serve(g):
        begin(g + 3)
        if g + 1 < chunks:
            px_copy(g + 1, c).start()
        own_part(g + 2)
        pass_partner(g + 2)
        pass_lines(g + 1)

    for g in range(3):
        begin(g)
    own_part(0)

    @pl.loop(1, nh)
    def _(d):
        tok_copy(d, head, next_head(d)).start()

    own = pltpu.make_async_copy(tok_ref, tok.at[own_rows(c), features(head)], tok_own)
    own.start()
    row_copy(c).start()
    px_copy(0, c).start()
    pass_partner(0)
    own_part(1)
    pass_lines(0)
    pass_partner(1)
    row_copy(1 - c).wait_recv()
    tail_out[...] = jnp.broadcast_to(most(row[1]), tail_out.shape)

    @pl.loop(0, span)
    def _(j):
        tail_copy(j).start()

    for i in range(2 * chunks):
        col[pl.ds(i * CHUNK, CHUNK), :] = jnp.broadcast_to(ids_of(i), (HEAD_DIM, CHUNK)).T

    serve(0)
    own.wait()

    @pl.loop(1, nh)
    def _(d):
        tok_copy(d, prior_head(d), head).wait_recv()

    finish(0)
    project_own(0)
    serve(1)
    if halves == 1:
        for i in range(3, chunks):
            px_copy(i, c).start()
        finish(1)
        project_own(1)
        for i in range(chunks):
            pass_piece(i)
            use_piece(i, (0, 1))
        own_states(0)
        add_states(0)
        queries = (2,)
    else:
        for g in range(1, 4):
            if g > 1:
                serve(g)
            pass_piece(g - 1)
            finish(g)
            project_own(g)
            if g > 1:
                project_pieces(g, g - 1)
            use_piece(g - 1, range(g + 1))
        for i in range(3, chunks):
            if i > 3:
                px_copy(i, c).start()
            pass_piece(i)
        serve(4)
        for i in range(3, chunks):
            use_piece(i, range(4))
        own_states(0)
        add_states(0)
        attend_partner(2, False)
        serve(5)
        attend_own(2, False)
        finish(4)
        project_own(4)
        project_pieces(4, chunks)
        own_states(1)
        queries = (5, 6)
    for g in queries:
        finish(g)
        if g == 5:
            add_states(1)
        attend_partner(g, True)
        attend_own(g, True)

    for g in range(last + 1):
        x_copy(g, c).wait_send()

        @pl.loop(1, lines)
        def _(d):
            for far in (False, True):
                z_copy(g, d, far, a, lax.rem(a + d, lines)).wait_send()

        @pl.loop(0, lines)
        def _(d):
            for far in (False, True):
                y_copy(g, d, far, b).wait_send()

    row_copy(c).wait_send()

    @pl.loop(1, nh)
    def _(d):
        tok_copy(d, head, next_head(d)).wait_send()

    for i in range(chunks):
        px_copy(i, c).wait_send()

        @pl.loop(1, nh)
        def _(d):
            ph_copy(i, d, head, next_head(d)).wait_send()

    @pl.loop(0, span)
    def _(j):
        tail_copy(j).wait_send()
        for half in range(halves):
            state_copy(half, j).wait_send()

    for g, (which, _, _) in enumerate(groups):
        if which == 0:
            out_keep(g).wait()

            @pl.loop(0, chunks)
            def _(i):
                out_copy(g, i, c).wait_send()
                out_copy(g, i, 1 - c).wait_recv()


def per_device(n, nh, tokens, w_qkv, out_gain, seg_ids):
    rows, width = tokens.shape
    part_rows, own_cols = w_qkv.shape[1:]
    cols = own_cols // 2
    heads = cols // HEAD_DIM
    plan = groups_of(heads)
    halves = heads // plan[0][2]
    lines, span, chunks = n // 4, n // 8, rows // CHUNK
    groups = len(plan)
    vmem = pl.BlockSpec(memory_space=pltpu.VMEM)
    hbm = pl.BlockSpec(memory_space=pl.ANY)
    dma = pltpu.SemaphoreType.DMA
    state = (heads, HEAD_DIM, HEAD_DIM)
    return pl.pallas_call(
        functools.partial(kernel, n, nh, plan),
        out_shape=jax.ShapeDtypeStruct((rows, own_cols), BF16),
        in_specs=[hbm, vmem, vmem, vmem],
        out_specs=hbm,
        scratch_shapes=[
            [pltpu.VMEM((lines, 2, 2, part_rows, count * HEAD_DIM), BF16) for _, _, count in plan],
            [pltpu.VMEM((part_rows, count * HEAD_DIM), BF16) for _, _, count in plan],
            pltpu.VMEM((2 * rows, width * nh), BF16),
            pltpu.VMEM((3, 2 * rows, cols), BF16),
            pltpu.VMEM((2 * rows, cols), BF16),
            pltpu.VMEM((2 * chunks,) + state, F32),
            pltpu.VMEM(state, F32),
            pltpu.VMEM(state, BF16),
            pltpu.VMEM((span,) + state, BF16),
            pltpu.VMEM((2, 1, rows), jnp.int32),
            pltpu.VMEM((2 * rows, HEAD_DIM), jnp.int32),
            pltpu.VMEM((8, HEAD_DIM), jnp.int32),
            pltpu.VMEM((span, 8, HEAD_DIM), jnp.int32),
            dma((groups,)), dma((groups,)),
            dma((groups, 2 * lines - 2)), dma((groups, 2 * lines - 2)),
            dma((groups, 2 * lines)), dma((groups, 2 * lines)),
            dma((nh - 1,)), dma((nh - 1,)), dma,
            dma((chunks,)), dma((chunks,)),
            dma((chunks, nh - 1)), dma((chunks, nh - 1)),
            dma((halves, span)), dma((halves, span)),
            dma((span,)), dma((span,)),
            dma, dma,
            dma((groups, chunks)), dma((groups, chunks)), dma((groups,)),
        ],
        compiler_params=pltpu.CompilerParams(
            collective_id=0, has_side_effects=True, vmem_limit_bytes=56 * 1024 * 1024
        ),
        cost_estimate=pl.CostEstimate(
            flops=2 * rows * width * nh * own_cols * 3,
            bytes_accessed=4 * rows * width, transcendentals=rows * own_cols,
        ),
    )(tokens, w_qkv, out_gain.reshape(1, own_cols), seg_ids.reshape(1, rows))


def solution(mesh):
    placed = (P("ctx", "head"), P(None, "ctx", "head"), P("head"), P("ctx"))
    sizes = (mesh.shape["ctx"], mesh.shape["head"])
    return jax.shard_map(
        functools.partial(per_device, *sizes),
        mesh=mesh, in_specs=placed, out_specs=P("ctx", "head"), check_vma=False,
    )
```

```python
import functools

import jax
import jax.numpy as jnp
from jax import lax
from jax.experimental import pallas as pl
from jax.experimental.pallas import tpu as pltpu
from jax.sharding import PartitionSpec as P

HEAD_DIM = 128
CHUNK = 256
MESH = pl.DeviceIdType.MESH
F32, BF16 = jnp.float32, jnp.bfloat16


def groups_of(heads):
    if heads % 4:
        return ((1, 0, heads), (2, 0, heads), (0, 0, heads))
    half = heads // 2
    first = tuple((which, 0, half) for which in (1, 2, 0))
    second = tuple((which, half, half) for which in (1, 2))
    return first + second + ((0, half, half // 2), (0, half + half // 2, half // 2))


def dot(left, right, dims=((1,), (0,))):
    return lax.dot_general(left, right, (dims, ((), ())), preferred_element_type=F32)


def kernel(
    n, nh, groups, tok_ref, w_ref, gain_ref, row_ref, out_ref, wbufs, wouts, tok, qkv, outs, early, outers, local, incoming, state_out, state_got, row, col, tail_out, tail_got,
    x_send, x_recv, z_send, z_recv, y_send, y_recv,
    tok_send, tok_recv, tok_own, px_send, px_recv, ph_send, ph_recv,
    st_send, st_recv, tl_send, tl_recv, row_send, row_recv, out_send, out_recv, out_own,
):
    lines = n // 4
    pairs = n // 2
    span = n // 8
    rows, width = tok_ref.shape[0], tok_ref.shape[1]
    depth = n * w_ref.shape[1]
    all_heads = w_ref.shape[2] // 2 // HEAD_DIM
    heads = groups[0][2]
    halves = all_heads // heads
    chunks = rows // CHUNK
    last = len(groups) - 1
    ctx, head = lax.axis_index("ctx"), lax.axis_index("head")
    a, b, c = ctx // 4, (ctx // 2) % 2, ctx % 2
    pair = ctx // 2

    def place(a_, b_, c_):
        return (a_ * 4 + b_ * 2 + c_, head)

    def line_at(step):
        return lax.rem(a - step + lines, lines)

    barrier = pltpu.get_barrier_semaphore()

    def greet(where):
        pl.semaphore_signal(barrier, inc=1, device_id=where, device_id_type=MESH)

    greet(place(a, b, 1 - c))
    greet(place(a, 1 - b, c))

    @pl.loop(1, lines)
    def _(d):
        greet(place(lax.rem(a + d, lines), b, c))

    @pl.loop(1, span + 1)
    def _(d):
        greet((lax.rem(pair + d, pairs) * 2 + c, head))
        greet((lax.rem(pair - d + pairs, pairs) * 2 + c, head))

    @pl.loop(1, nh)
    def _(d):
        greet((ctx, lax.rem(head + d, nh)))

    for g, (which, first, count) in enumerate(groups):
        span_of = count * HEAD_DIM
        keep = pl.ds(pl.multiple_of((c * all_heads + first) * HEAD_DIM, 128), span_of)
        give = pl.ds(pl.multiple_of(((1 - c) * all_heads + first) * HEAD_DIM, 128), span_of)
        wbufs[g][a, b, c] = w_ref[which, :, keep]
        wouts[g][...] = w_ref[which, :, give]
    row[c] = row_ref[...]

    pl.semaphore_wait(barrier, 2 + (lines - 1) + 2 * span + (nh - 1))

    def remote(src, dst, send, recv, where):
        return pltpu.make_async_remote_copy(
            src_ref=src, dst_ref=dst, send_sem=send, recv_sem=recv,
            device_id=where, device_id_type=MESH,
        )

    def x_copy(g, c_):
        return remote(
            wouts[g], wbufs[g].at[a, b, c_], x_send.at[g], x_recv.at[g], place(a, b, 1 - c)
        )

    def z_copy(g, d, far, slot_line, to_line):
        slot = wbufs[g].at[slot_line, b, 1 - c if far else c]
        at = d - 1 + (lines - 1 if far else 0)
        return remote(slot, slot, z_send.at[g, at], z_recv.at[g, at], place(to_line, b, c))

    def y_copy(g, k, far, b_):
        slot = wbufs[g].at[line_at(k), b_, 1 - c if far else c]
        at = k + (lines if far else 0)
        return remote(slot, slot, y_send.at[g, at], y_recv.at[g, at], place(a, 1 - b, c))

    def features(of):
        return pl.ds(pl.multiple_of(of * width, 128), width)

    def own_rows(of):
        return pl.ds(pl.multiple_of(of * rows, CHUNK), rows)

    def piece(of, i):
        return pl.ds(pl.multiple_of(of * rows + i * CHUNK, CHUNK), CHUNK)

    def tok_copy(d, of, to):
        there = tok.at[own_rows(c), features(of)]
        return remote(tok_ref, there, tok_send.at[d - 1], tok_recv.at[d - 1], (ctx, to))

    def px_copy(i, of):
        return remote(
            tok_ref.at[pl.ds(i * CHUNK, CHUNK)], tok.at[piece(of, i), features(head)],
            px_send.at[i], px_recv.at[i], place(a, b, 1 - c),
        )

    def ph_copy(i, d, of, to):
        there = tok.at[piece(1 - c, i), features(of)]
        return remote(there, there, ph_send.at[i, d - 1], ph_recv.at[i, d - 1], (ctx, to))

    def state_copy(half, j):
        part = pl.ds(half * heads, heads)
        return remote(
            state_out.at[part], state_got.at[j, part], st_send.at[half, j], st_recv.at[half, j],
            (lax.rem(pair + j + 1, pairs) * 2 + c, head),
        )

    def tail_copy(j):
        return remote(
            tail_out, tail_got.at[j], tl_send.at[j], tl_recv.at[j],
            (lax.rem(pair + j + 1, pairs) * 2 + c, head),
        )

    def row_copy(c_):
        return remote(row.at[c_], row.at[c_], row_send, row_recv, place(a, b, 1 - c))

    def lanes_of(g):
        return pl.ds(groups[g][1] * HEAD_DIM, groups[g][2] * HEAD_DIM)

    def out_lanes(g, of):
        start = pl.multiple_of((of * all_heads + groups[g][1]) * HEAD_DIM, 128)
        return pl.ds(start, groups[g][2] * HEAD_DIM)

    def out_copy(g, i, of):
        at = pl.ds(pl.multiple_of(i * CHUNK, CHUNK), CHUNK)
        return remote(
            outs.at[piece(1 - c, i), lanes_of(g)], out_ref.at[at, out_lanes(g, of)],
            out_send.at[g, i], out_recv.at[g, i], place(a, b, 1 - c),
        )

    def out_keep(g):
        return pltpu.make_async_copy(
            outs.at[own_rows(c), lanes_of(g)], out_ref.at[:, out_lanes(g, c)], out_own.at[g]
        )

    def next_head(d):
        return lax.rem(head + d, nh)

    def prior_head(d):
        return lax.rem(head - d + nh, nh)

    def spread(g, far):
        y_copy(g, 0, far, b).start()

        @pl.loop(1, lines)
        def _(d):
            z_copy(g, d, far, a, lax.rem(a + d, lines)).start()

    def begin(g):
        if g <= last:
            x_copy(g, c).start()

    def own_part(g):
        if g <= last:
            spread(g, False)

    def pass_partner(g):
        if g <= last:
            x_copy(g, 1 - c).wait_recv()
            spread(g, True)

    def pass_lines(g):
        for far in (False, True):
            @pl.loop(1, lines if g <= last else 1)
            def _(d):
                z_copy(g, d, far, line_at(d), a).wait_recv()
                y_copy(g, d, far, b).start()

    def finish(g):
        @pl.loop(0, lines)
        def _(d):
            for far in (False, True):
                y_copy(g, d, far, 1 - b).wait_recv()

    def project(g, of, i, height):
        which = groups[g][0]
        part = pl.ds(pl.multiple_of(of * rows + i * height, height), height)
        got = dot(tok[part, :], wbufs[g][...].reshape(depth, groups[g][2] * HEAD_DIM)).astype(BF16)
        if which < 2:
            wide = got.astype(F32)
            got = jnp.where(wide > 0.0, wide + 1.0, jnp.exp(jnp.minimum(wide, 0.0))).astype(BF16)
        qkv[which, part, lanes_of(g)] = got

    def project_own(g):
        @pl.loop(0, rows // 512)
        def _(i):
            project(g, c, i, 512)

    def ids_of(i):
        return row[i // chunks, :, (i % chunks) * CHUNK:(i % chunks + 1) * CHUNK]

    def least(ids):
        return jnp.min(ids, axis=1, keepdims=True)

    def most(ids):
        return jnp.max(ids, axis=1, keepdims=True)

    def outer(half, of, i):
        part = piece(of, i)
        tail = most(row[of, :, pl.ds(pl.multiple_of(i * CHUNK, CHUNK), CHUNK)])
        in_tail = col[part, 0:1] == tail
        for at in range(half * heads, (half + 1) * heads):
            lanes = pl.ds(at * HEAD_DIM, HEAD_DIM)
            keys = qkv[1, part, lanes]
            keys = jnp.where(in_tail, keys, jnp.zeros_like(keys))
            outers[of * chunks + i, at] = dot(keys, qkv[2, part, lanes], ((0,), (0,)))

    def outer_all(half, of):
        @pl.loop(0, chunks)
        def _(i):
            outer(half, of, i)

    def own_states(half):
        for h in range(heads):
            at = half * heads + h
            state = jnp.zeros((HEAD_DIM, HEAD_DIM), F32)
            before = None
            for i in range(2 * chunks):
                first, tail = least(ids_of(i)), most(ids_of(i))
                if i > 0:
                    state = jnp.where(before == first, state, 0.0)
                local[i, at] = state
                state = jnp.where(first == tail, state, 0.0) + outers[i, at]
                before = tail
            state_out[at] = state.astype(BF16)

        @pl.loop(0, span)
        def _(j):
            state_copy(half, j).start()

    def add_states(half):
        first = least(ids_of(0))
        own = range(half * heads, (half + 1) * heads)
        for at in own:
            incoming[at] = jnp.zeros((HEAD_DIM, HEAD_DIM), F32)

        @pl.loop(0, span)
        def _(j):
            if half == 0:
                tail_copy(j).wait_recv()
            state_copy(half, j).wait_recv()
            ids = tail_got[j][0:1, :] + jnp.where(pair > j, 0, -1000)
            linked = ids == first
            for at in own:
                incoming[at] += jnp.where(linked, state_got[j, at].astype(F32), 0.0)

        for i in range(2 * chunks):
            here = least(ids_of(i))
            for at in own:
                local[i, at] += jnp.where(here == first, incoming[at], 0.0)

    def heads_of(g):
        return range(groups[g][1], groups[g][1] + groups[g][2])

    def local_parts(g, of, i):
        part = piece(of, i)
        ids_row = row[of, :, pl.ds(pl.multiple_of(i * CHUNK, CHUNK), CHUNK)]
        later = lax.broadcasted_iota(jnp.int32, (CHUNK, CHUNK), 0)
        sooner = lax.broadcasted_iota(jnp.int32, (CHUNK, CHUNK), 1)
        visible = (sooner <= later) & (ids_row == col[part, 0:1])
        totals = []
        for at in heads_of(g):
            lanes = pl.ds(at * HEAD_DIM, HEAD_DIM)
            scores = dot(qkv[0, part, lanes], qkv[1, part, lanes], ((1,), (1,)))
            scores = jnp.where(visible, scores, 0.0).astype(BF16)
            totals.append(dot(scores, qkv[2, part, lanes]))
        return totals

    def keep_local(g, of, i):
        for at, total in zip(heads_of(g), local_parts(g, of, i)):
            early[piece(of, i), pl.ds(at * HEAD_DIM, HEAD_DIM)] = total

    def attend(g, of, i, fresh):
        part = piece(of, i)
        ids_row = row[of, :, pl.ds(pl.multiple_of(i * CHUNK, CHUNK), CHUNK)]
        reached = col[part, 0:1] == least(ids_row)
        if fresh:
            totals = local_parts(g, of, i)
        else:
            totals = [early[part, pl.ds(at * HEAD_DIM, HEAD_DIM)] for at in heads_of(g)]
        for at, total in zip(heads_of(g), totals):
            lanes = pl.ds(at * HEAD_DIM, HEAD_DIM)
            prefix = dot(qkv[0, part, lanes], local[of * chunks + i, at].astype(BF16))
            total = total + jnp.where(reached, prefix, 0.0)
            scale = lax.rsqrt(jnp.mean(total * total, axis=1, keepdims=True) + 1e-05)
            gain = gain_ref[:, pl.ds(pl.multiple_of((c * all_heads + at) * HEAD_DIM, 128), HEAD_DIM)]
            outs[part, lanes] = (total * scale * gain).astype(BF16)

    def attend_partner(g, fresh):
        @pl.loop(0, rows // 512)
        def _(i):
            if fresh:
                project(g, 1 - c, i, 512)
            for part in range(512 // CHUNK):
                attend(g, 1 - c, i * (512 // CHUNK) + part, fresh)
            for part in range(512 // CHUNK):
                out_copy(g, i * (512 // CHUNK) + part, c).start()

    def attend_own(g, fresh):
        @pl.loop(0, rows // 512)
        def _(i):
            if fresh:
                project(g, c, i, 512)
            for part in range(512 // CHUNK):
                attend(g, c, i * (512 // CHUNK) + part, fresh)

        out_keep(g).start()

    def pass_piece(i):
        px_copy(i, 1 - c).wait_recv()

        @pl.loop(1, nh)
        def _(d):
            ph_copy(i, d, head, next_head(d)).start()

    def use_piece(i, of_groups):
        @pl.loop(1, nh)
        def _(d):
            ph_copy(i, d, prior_head(d), head).wait_recv()

        for g in of_groups:
            project(g, 1 - c, i, CHUNK)

    def project_pieces(g, count):
        @pl.loop(0, count)
        def _(i):
            project(g, 1 - c, i, CHUNK)

    def serve(g):
        begin(g + 3)
        if g + 1 < chunks:
            px_copy(g + 1, c).start()
        own_part(g + 2)
        pass_partner(g + 2)
        pass_lines(g + 1)

    for g in range(3):
        begin(g)
    own_part(0)

    @pl.loop(1, nh)
    def _(d):
        tok_copy(d, head, next_head(d)).start()

    own = pltpu.make_async_copy(tok_ref, tok.at[own_rows(c), features(head)], tok_own)
    own.start()
    row_copy(c).start()
    px_copy(0, c).start()
    pass_partner(0)
    own_part(1)
    pass_lines(0)
    pass_partner(1)
    row_copy(1 - c).wait_recv()
    tail_out[...] = jnp.broadcast_to(most(row[1]), tail_out.shape)

    @pl.loop(0, span)
    def _(j):
        tail_copy(j).start()

    for i in range(2 * chunks):
        col[pl.ds(i * CHUNK, CHUNK), :] = jnp.broadcast_to(ids_of(i), (HEAD_DIM, CHUNK)).T

    serve(0)
    own.wait()

    @pl.loop(1, nh)
    def _(d):
        tok_copy(d, prior_head(d), head).wait_recv()

    finish(0)
    project_own(0)
    serve(1)
    if halves == 1:
        for i in range(3, chunks):
            px_copy(i, c).start()
        finish(1)
        project_own(1)
        for i in range(chunks):
            pass_piece(i)
            use_piece(i, (0, 1))
        outer_all(0, c)
        outer_all(0, 1 - c)
        own_states(0)
        add_states(0)
        queries = (2,)
    else:
        for g in range(1, 4):
            if g > 1:
                serve(g)
            pass_piece(g - 1)
            finish(g)
            project_own(g)
            if g > 1:
                project_pieces(g, g - 1)
            if g == 1:
                outer_all(0, c)
            elif g == 2:
                @pl.loop(0, chunks)
                def _(i):
                    keep_local(2, c, i)

                keep_local(2, 1 - c, 0)
            use_piece(g - 1, range(g + 1))
            outer(0, 1 - c, g - 1)
            if g > 1:
                keep_local(2, 1 - c, g - 1)
        for i in range(3, chunks):
            if i > 3:
                px_copy(i, c).start()
            pass_piece(i)
        serve(4)
        for i in range(3, chunks):
            use_piece(i, range(4))
            outer(0, 1 - c, i)
            keep_local(2, 1 - c, i)
        own_states(0)
        add_states(0)
        attend_partner(2, False)
        serve(5)
        attend_own(2, False)
        finish(4)
        project_own(4)
        project_pieces(4, chunks)
        outer_all(1, c)
        outer_all(1, 1 - c)
        own_states(1)
        queries = (5, 6)
    for g in queries:
        finish(g)
        if g == 5:
            add_states(1)
        attend_partner(g, True)
        attend_own(g, True)

    for g in range(last + 1):
        x_copy(g, c).wait_send()

        @pl.loop(1, lines)
        def _(d):
            for far in (False, True):
                z_copy(g, d, far, a, lax.rem(a + d, lines)).wait_send()

        @pl.loop(0, lines)
        def _(d):
            for far in (False, True):
                y_copy(g, d, far, b).wait_send()

    row_copy(c).wait_send()

    @pl.loop(1, nh)
    def _(d):
        tok_copy(d, head, next_head(d)).wait_send()

    for i in range(chunks):
        px_copy(i, c).wait_send()

        @pl.loop(1, nh)
        def _(d):
            ph_copy(i, d, head, next_head(d)).wait_send()

    @pl.loop(0, span)
    def _(j):
        tail_copy(j).wait_send()
        for half in range(halves):
            state_copy(half, j).wait_send()

    for g, (which, _, _) in enumerate(groups):
        if which == 0:
            out_keep(g).wait()

            @pl.loop(0, chunks)
            def _(i):
                out_copy(g, i, c).wait_send()
                out_copy(g, i, 1 - c).wait_recv()


def per_device(n, nh, tokens, w_qkv, out_gain, seg_ids):
    rows, width = tokens.shape
    part_rows, own_cols = w_qkv.shape[1:]
    cols = own_cols // 2
    heads = cols // HEAD_DIM
    plan = groups_of(heads)
    halves = heads // plan[0][2]
    lines, span, chunks = n // 4, n // 8, rows // CHUNK
    groups = len(plan)
    vmem = pl.BlockSpec(memory_space=pltpu.VMEM)
    hbm = pl.BlockSpec(memory_space=pl.ANY)
    dma = pltpu.SemaphoreType.DMA
    state = (heads, HEAD_DIM, HEAD_DIM)
    return pl.pallas_call(
        functools.partial(kernel, n, nh, plan),
        out_shape=jax.ShapeDtypeStruct((rows, own_cols), BF16),
        in_specs=[hbm, vmem, vmem, vmem],
        out_specs=hbm,
        scratch_shapes=[
            [pltpu.VMEM((lines, 2, 2, part_rows, count * HEAD_DIM), BF16) for _, _, count in plan],
            [pltpu.VMEM((part_rows, count * HEAD_DIM), BF16) for _, _, count in plan],
            pltpu.VMEM((2 * rows, width * nh), BF16),
            pltpu.VMEM((3, 2 * rows, cols), BF16),
            pltpu.VMEM((2 * rows, cols), BF16),
            pltpu.VMEM((2 * rows, plan[0][2] * HEAD_DIM), F32),
            pltpu.VMEM((2 * chunks,) + state, F32),
            pltpu.VMEM((2 * chunks,) + state, F32),
            pltpu.VMEM(state, F32),
            pltpu.VMEM(state, BF16),
            pltpu.VMEM((span,) + state, BF16),
            pltpu.VMEM((2, 1, rows), jnp.int32),
            pltpu.VMEM((2 * rows, HEAD_DIM), jnp.int32),
            pltpu.VMEM((8, HEAD_DIM), jnp.int32),
            pltpu.VMEM((span, 8, HEAD_DIM), jnp.int32),
            dma((groups,)), dma((groups,)),
            dma((groups, 2 * lines - 2)), dma((groups, 2 * lines - 2)),
            dma((groups, 2 * lines)), dma((groups, 2 * lines)),
            dma((nh - 1,)), dma((nh - 1,)), dma,
            dma((chunks,)), dma((chunks,)),
            dma((chunks, nh - 1)), dma((chunks, nh - 1)),
            dma((halves, span)), dma((halves, span)),
            dma((span,)), dma((span,)),
            dma, dma,
            dma((groups, chunks)), dma((groups, chunks)), dma((groups,)),
        ],
        compiler_params=pltpu.CompilerParams(
            collective_id=0, has_side_effects=True, vmem_limit_bytes=44 * 1024 * 1024
        ),
        cost_estimate=pl.CostEstimate(
            flops=2 * rows * width * nh * own_cols * 3,
            bytes_accessed=4 * rows * width, transcendentals=rows * own_cols,
        ),
    )(tokens, w_qkv, out_gain.reshape(1, own_cols), seg_ids.reshape(1, rows))


def solution(mesh):
    placed = (P("ctx", "head"), P(None, "ctx", "head"), P("head"), P("ctx"))
    sizes = (mesh.shape["ctx"], mesh.shape["head"])
    return jax.shard_map(
        functools.partial(per_device, *sizes),
        mesh=mesh, in_specs=placed, out_specs=P("ctx", "head"), check_vma=False,
    )
```

```python
import functools

import jax
import jax.numpy as jnp
from jax import lax
from jax.experimental import pallas as pl
from jax.experimental.pallas import tpu as pltpu
from jax.sharding import PartitionSpec as P

HEAD_DIM = 128
CHUNK = 256
MESH = pl.DeviceIdType.MESH
F32, BF16 = jnp.float32, jnp.bfloat16


def groups_of(heads):
    if heads % 4:
        return ((1, 0, heads), (2, 0, heads), (0, 0, heads))
    half = heads // 2
    first = tuple((which, 0, half) for which in (1, 2, 0))
    second = tuple((which, half, half) for which in (1, 2))
    return first + second + ((0, half, half // 2), (0, half + half // 2, half // 2))


def dot(left, right, dims=((1,), (0,))):
    return lax.dot_general(left, right, (dims, ((), ())), preferred_element_type=F32)


def kernel(
    n, nh, groups, tok_ref, w_ref, gain_ref, row_ref, out_ref, wbufs, wouts, tok, qkv, outs, early, outers, local, incoming, state_out, state_got, row, col, tail_out, tail_got,
    x_send, x_recv, z_send, z_recv, y_send, y_recv,
    tok_send, tok_recv, tok_own, px_send, px_recv, ph_send, ph_recv,
    st_send, st_recv, tl_send, tl_recv, row_send, row_recv, out_send, out_recv, out_own,
):
    lines = n // 4
    pairs = n // 2
    span = n // 8
    rows, width = tok_ref.shape[0], tok_ref.shape[1]
    depth = n * w_ref.shape[1]
    all_heads = w_ref.shape[2] // 2 // HEAD_DIM
    heads = groups[0][2]
    halves = all_heads // heads
    chunks = rows // CHUNK
    last = len(groups) - 1
    ctx, head = lax.axis_index("ctx"), lax.axis_index("head")
    a, b, c = ctx // 4, (ctx // 2) % 2, ctx % 2
    pair = ctx // 2

    def place(a_, b_, c_):
        return (a_ * 4 + b_ * 2 + c_, head)

    def line_at(step):
        return lax.rem(a - step + lines, lines)

    barrier = pltpu.get_barrier_semaphore()

    def greet(where):
        pl.semaphore_signal(barrier, inc=1, device_id=where, device_id_type=MESH)

    greet(place(a, b, 1 - c))
    greet(place(a, 1 - b, c))

    @pl.loop(1, lines)
    def _(d):
        greet(place(lax.rem(a + d, lines), b, c))

    @pl.loop(1, span + 1)
    def _(d):
        greet((lax.rem(pair + d, pairs) * 2 + c, head))
        greet((lax.rem(pair - d + pairs, pairs) * 2 + c, head))

    @pl.loop(1, nh)
    def _(d):
        greet((ctx, lax.rem(head + d, nh)))

    for g, (which, first, count) in enumerate(groups):
        span_of = count * HEAD_DIM
        keep = pl.ds(pl.multiple_of((c * all_heads + first) * HEAD_DIM, 128), span_of)
        give = pl.ds(pl.multiple_of(((1 - c) * all_heads + first) * HEAD_DIM, 128), span_of)
        wbufs[g][a, b, c] = w_ref[which, :, keep]
        wouts[g][...] = w_ref[which, :, give]
    row[c] = row_ref[...]

    pl.semaphore_wait(barrier, 2 + (lines - 1) + 2 * span + (nh - 1))

    def remote(src, dst, send, recv, where):
        return pltpu.make_async_remote_copy(
            src_ref=src, dst_ref=dst, send_sem=send, recv_sem=recv,
            device_id=where, device_id_type=MESH,
        )

    def x_copy(g, c_):
        return remote(
            wouts[g], wbufs[g].at[a, b, c_], x_send.at[g], x_recv.at[g], place(a, b, 1 - c)
        )

    def z_copy(g, d, far, slot_line, to_line):
        slot = wbufs[g].at[slot_line, b, 1 - c if far else c]
        at = d - 1 + (lines - 1 if far else 0)
        return remote(slot, slot, z_send.at[g, at], z_recv.at[g, at], place(to_line, b, c))

    def y_copy(g, k, far, b_):
        slot = wbufs[g].at[line_at(k), b_, 1 - c if far else c]
        at = k + (lines if far else 0)
        return remote(slot, slot, y_send.at[g, at], y_recv.at[g, at], place(a, 1 - b, c))

    def features(of):
        return pl.ds(pl.multiple_of(of * width, 128), width)

    def own_rows(of):
        return pl.ds(pl.multiple_of(of * rows, CHUNK), rows)

    def piece(of, i):
        return pl.ds(pl.multiple_of(of * rows + i * CHUNK, CHUNK), CHUNK)

    def tok_copy(d, of, to):
        there = tok.at[own_rows(c), features(of)]
        return remote(tok_ref, there, tok_send.at[d - 1], tok_recv.at[d - 1], (ctx, to))

    def px_copy(i, of):
        return remote(
            tok_ref.at[pl.ds(i * CHUNK, CHUNK)], tok.at[piece(of, i), features(head)],
            px_send.at[i], px_recv.at[i], place(a, b, 1 - c),
        )

    def ph_copy(i, d, of, to):
        there = tok.at[piece(1 - c, i), features(of)]
        return remote(there, there, ph_send.at[i, d - 1], ph_recv.at[i, d - 1], (ctx, to))

    def state_copy(half, j):
        part = pl.ds(half * heads, heads)
        return remote(
            state_out.at[part], state_got.at[j, part], st_send.at[half, j], st_recv.at[half, j],
            (lax.rem(pair + j + 1, pairs) * 2 + c, head),
        )

    def tail_copy(j):
        return remote(
            tail_out, tail_got.at[j], tl_send.at[j], tl_recv.at[j],
            (lax.rem(pair + j + 1, pairs) * 2 + c, head),
        )

    def row_copy(c_):
        return remote(row.at[c_], row.at[c_], row_send, row_recv, place(a, b, 1 - c))

    def lanes_of(g):
        return pl.ds(groups[g][1] * HEAD_DIM, groups[g][2] * HEAD_DIM)

    def out_lanes(g, of):
        start = pl.multiple_of((of * all_heads + groups[g][1]) * HEAD_DIM, 128)
        return pl.ds(start, groups[g][2] * HEAD_DIM)

    def out_copy(g, i, of):
        at = pl.ds(pl.multiple_of(i * CHUNK, CHUNK), CHUNK)
        return remote(
            outs.at[piece(1 - c, i), lanes_of(g)], out_ref.at[at, out_lanes(g, of)],
            out_send.at[g, i], out_recv.at[g, i], place(a, b, 1 - c),
        )

    def out_keep(g):
        return pltpu.make_async_copy(
            outs.at[own_rows(c), lanes_of(g)], out_ref.at[:, out_lanes(g, c)], out_own.at[g]
        )

    def next_head(d):
        return lax.rem(head + d, nh)

    def prior_head(d):
        return lax.rem(head - d + nh, nh)

    def spread(g, far):
        y_copy(g, 0, far, b).start()

        @pl.loop(1, lines)
        def _(d):
            z_copy(g, d, far, a, lax.rem(a + d, lines)).start()

    def begin(g):
        if g <= last:
            x_copy(g, c).start()

    def own_part(g):
        if g <= last:
            spread(g, False)

    def pass_partner(g):
        if g <= last:
            x_copy(g, 1 - c).wait_recv()
            spread(g, True)

    def line_steps(g):
        def step(far, d):
            z_copy(g, d, far, line_at(d), a).wait_recv()
            y_copy(g, d, far, b).start()

        return [
            functools.partial(step, far, d) for far in (False, True) for d in range(1, lines)
        ]

    def weave(steps, tasks, at_once=1):
        steps, tasks = list(steps), list(tasks)
        while steps or tasks:
            for step in steps[:at_once]:
                step()
            steps = steps[at_once:]
            if tasks:
                tasks.pop(0)()

    def finish(g):
        @pl.loop(0, lines)
        def _(d):
            for far in (False, True):
                y_copy(g, d, far, 1 - b).wait_recv()

    def project(g, of, i, height):
        which = groups[g][0]
        part = pl.ds(pl.multiple_of(of * rows + i * height, height), height)
        got = dot(tok[part, :], wbufs[g][...].reshape(depth, groups[g][2] * HEAD_DIM)).astype(BF16)
        if which < 2:
            wide = got.astype(F32)
            got = jnp.where(wide > 0.0, wide + 1.0, jnp.exp(jnp.minimum(wide, 0.0))).astype(BF16)
        qkv[which, part, lanes_of(g)] = got

    def project_own(g):
        @pl.loop(0, rows // 512)
        def _(i):
            project(g, c, i, 512)

    def ids_of(i):
        return row[i // chunks, :, (i % chunks) * CHUNK:(i % chunks + 1) * CHUNK]

    def least(ids):
        return jnp.min(ids, axis=1, keepdims=True)

    def most(ids):
        return jnp.max(ids, axis=1, keepdims=True)

    def outer(half, of, i):
        part = piece(of, i)
        tail = most(row[of, :, pl.ds(pl.multiple_of(i * CHUNK, CHUNK), CHUNK)])
        in_tail = col[part, 0:1] == tail
        for at in range(half * heads, (half + 1) * heads):
            lanes = pl.ds(at * HEAD_DIM, HEAD_DIM)
            keys = qkv[1, part, lanes]
            keys = jnp.where(in_tail, keys, jnp.zeros_like(keys))
            outers[of * chunks + i, at] = dot(keys, qkv[2, part, lanes], ((0,), (0,)))

    def outer_all(half, of):
        @pl.loop(0, chunks)
        def _(i):
            outer(half, of, i)

    def own_states(half):
        for h in range(heads):
            at = half * heads + h
            state = jnp.zeros((HEAD_DIM, HEAD_DIM), F32)
            before = None
            for i in range(2 * chunks):
                first, tail = least(ids_of(i)), most(ids_of(i))
                if i > 0:
                    state = jnp.where(before == first, state, 0.0)
                local[i, at] = state
                state = jnp.where(first == tail, state, 0.0) + outers[i, at]
                before = tail
            state_out[at] = state.astype(BF16)

        @pl.loop(0, span)
        def _(j):
            state_copy(half, j).start()

    def add_states(half):
        first = least(ids_of(0))
        own = range(half * heads, (half + 1) * heads)
        for at in own:
            incoming[at] = jnp.zeros((HEAD_DIM, HEAD_DIM), F32)

        @pl.loop(0, span)
        def _(j):
            if half == 0:
                tail_copy(j).wait_recv()
            state_copy(half, j).wait_recv()
            ids = tail_got[j][0:1, :] + jnp.where(pair > j, 0, -1000)
            linked = ids == first
            for at in own:
                incoming[at] += jnp.where(linked, state_got[j, at].astype(F32), 0.0)

        for i in range(2 * chunks):
            here = least(ids_of(i))
            for at in own:
                local[i, at] += jnp.where(here == first, incoming[at], 0.0)

    def heads_of(g):
        return range(groups[g][1], groups[g][1] + groups[g][2])

    def local_parts(g, of, i):
        part = piece(of, i)
        ids_row = row[of, :, pl.ds(pl.multiple_of(i * CHUNK, CHUNK), CHUNK)]
        later = lax.broadcasted_iota(jnp.int32, (CHUNK, CHUNK), 0)
        sooner = lax.broadcasted_iota(jnp.int32, (CHUNK, CHUNK), 1)
        visible = (sooner <= later) & (ids_row == col[part, 0:1])
        totals = []
        for at in heads_of(g):
            lanes = pl.ds(at * HEAD_DIM, HEAD_DIM)
            scores = dot(qkv[0, part, lanes], qkv[1, part, lanes], ((1,), (1,)))
            scores = jnp.where(visible, scores, 0.0).astype(BF16)
            totals.append(dot(scores, qkv[2, part, lanes]))
        return totals

    def keep_local(g, of, i):
        for at, total in zip(heads_of(g), local_parts(g, of, i)):
            early[piece(of, i), pl.ds(at * HEAD_DIM, HEAD_DIM)] = total

    def attend(g, of, i, fresh):
        part = piece(of, i)
        ids_row = row[of, :, pl.ds(pl.multiple_of(i * CHUNK, CHUNK), CHUNK)]
        reached = col[part, 0:1] == least(ids_row)
        if fresh:
            totals = local_parts(g, of, i)
        else:
            totals = [early[part, pl.ds(at * HEAD_DIM, HEAD_DIM)] for at in heads_of(g)]
        for at, total in zip(heads_of(g), totals):
            lanes = pl.ds(at * HEAD_DIM, HEAD_DIM)
            prefix = dot(qkv[0, part, lanes], local[of * chunks + i, at].astype(BF16))
            total = total + jnp.where(reached, prefix, 0.0)
            scale = lax.rsqrt(jnp.mean(total * total, axis=1, keepdims=True) + 1e-05)
            gain = gain_ref[:, pl.ds(pl.multiple_of((c * all_heads + at) * HEAD_DIM, 128), HEAD_DIM)]
            outs[part, lanes] = (total * scale * gain).astype(BF16)

    def attend_partner(g, fresh):
        @pl.loop(0, rows // 512)
        def _(i):
            if fresh:
                project(g, 1 - c, i, 512)
            for part in range(512 // CHUNK):
                attend(g, 1 - c, i * (512 // CHUNK) + part, fresh)
            for part in range(512 // CHUNK):
                out_copy(g, i * (512 // CHUNK) + part, c).start()

    def attend_own(g, fresh):
        @pl.loop(0, rows // 512)
        def _(i):
            if fresh:
                project(g, c, i, 512)
            for part in range(512 // CHUNK):
                attend(g, c, i * (512 // CHUNK) + part, fresh)

        out_keep(g).start()

    def pass_piece(i):
        px_copy(i, 1 - c).wait_recv()

        @pl.loop(1, nh)
        def _(d):
            ph_copy(i, d, head, next_head(d)).start()

    def use_piece(i, of_groups):
        @pl.loop(1, nh)
        def _(d):
            ph_copy(i, d, prior_head(d), head).wait_recv()

        for g in of_groups:
            project(g, 1 - c, i, CHUNK)

    def project_pieces(g, count):
        @pl.loop(0, count)
        def _(i):
            project(g, 1 - c, i, CHUNK)

    def serve(g):
        begin(g + 3)
        if g + 1 < chunks:
            px_copy(g + 1, c).start()
        own_part(g + 2)
        pass_partner(g + 2)

    for g in range(3):
        begin(g)
    own_part(0)

    @pl.loop(1, nh)
    def _(d):
        tok_copy(d, head, next_head(d)).start()

    own = pltpu.make_async_copy(tok_ref, tok.at[own_rows(c), features(head)], tok_own)
    own.start()
    row_copy(c).start()
    px_copy(0, c).start()
    pass_partner(0)
    own_part(1)
    weave(line_steps(0), ())
    pass_partner(1)
    row_copy(1 - c).wait_recv()
    tail_out[...] = jnp.broadcast_to(most(row[1]), tail_out.shape)

    @pl.loop(0, span)
    def _(j):
        tail_copy(j).start()

    for i in range(2 * chunks):
        col[pl.ds(i * CHUNK, CHUNK), :] = jnp.broadcast_to(ids_of(i), (HEAD_DIM, CHUNK)).T

    def do(function, *args):
        return functools.partial(function, *args)

    serve(0)
    own.wait()

    @pl.loop(1, nh)
    def _(d):
        tok_copy(d, prior_head(d), head).wait_recv()

    weave(line_steps(1), [do(finish, 0), do(project_own, 0)])
    serve(1)
    if halves == 1:
        for i in range(3, chunks):
            px_copy(i, c).start()
        weave(line_steps(2), [do(finish, 1), do(project_own, 1)])
        for i in range(chunks):
            pass_piece(i)
            use_piece(i, (0, 1))
        outer_all(0, c)
        outer_all(0, 1 - c)
        own_states(0)
        add_states(0)
        queries = (2,)
    else:
        def keep_own(g):
            @pl.loop(0, chunks)
            def _(i):
                keep_local(g, c, i)

        for g in range(1, 4):
            if g > 1:
                serve(g)
            pass_piece(g - 1)
            tasks = [do(finish, g), do(project_own, g)]
            if g > 1:
                tasks.append(do(project_pieces, g, g - 1))
            if g == 1:
                tasks.append(do(outer_all, 0, c))
            elif g == 2:
                tasks += [do(keep_own, 2), do(keep_local, 2, 1 - c, 0)]
            tasks += [do(use_piece, g - 1, range(g + 1)), do(outer, 0, 1 - c, g - 1)]
            if g > 1:
                tasks.append(do(keep_local, 2, 1 - c, g - 1))
            weave(line_steps(g + 1), tasks)
        for i in range(3, chunks):
            if i > 3:
                px_copy(i, c).start()
            pass_piece(i)
        serve(4)
        tasks = []
        for i in range(3, chunks):
            tasks += [
                do(use_piece, i, range(4)), do(outer, 0, 1 - c, i), do(keep_local, 2, 1 - c, i)
            ]
        tasks += [
            do(own_states, 0), do(finish, 4), do(project_own, 4), do(add_states, 0),
            do(attend_partner, 2, False), do(project_pieces, 4, chunks),
            do(outer_all, 1, c), do(outer_all, 1, 1 - c), do(own_states, 1),
            do(attend_own, 2, False),
        ]
        weave(line_steps(5) + line_steps(6), tasks, 2)
        queries = (5, 6)
    for g in queries:
        finish(g)
        if g == 5:
            add_states(1)
        attend_partner(g, True)
        attend_own(g, True)

    for g in range(last + 1):
        x_copy(g, c).wait_send()

        @pl.loop(1, lines)
        def _(d):
            for far in (False, True):
                z_copy(g, d, far, a, lax.rem(a + d, lines)).wait_send()

        @pl.loop(0, lines)
        def _(d):
            for far in (False, True):
                y_copy(g, d, far, b).wait_send()

    row_copy(c).wait_send()

    @pl.loop(1, nh)
    def _(d):
        tok_copy(d, head, next_head(d)).wait_send()

    for i in range(chunks):
        px_copy(i, c).wait_send()

        @pl.loop(1, nh)
        def _(d):
            ph_copy(i, d, head, next_head(d)).wait_send()

    @pl.loop(0, span)
    def _(j):
        tail_copy(j).wait_send()
        for half in range(halves):
            state_copy(half, j).wait_send()

    for g, (which, _, _) in enumerate(groups):
        if which == 0:
            out_keep(g).wait()

            @pl.loop(0, chunks)
            def _(i):
                out_copy(g, i, c).wait_send()
                out_copy(g, i, 1 - c).wait_recv()


def per_device(n, nh, tokens, w_qkv, out_gain, seg_ids):
    rows, width = tokens.shape
    part_rows, own_cols = w_qkv.shape[1:]
    cols = own_cols // 2
    heads = cols // HEAD_DIM
    plan = groups_of(heads)
    halves = heads // plan[0][2]
    lines, span, chunks = n // 4, n // 8, rows // CHUNK
    groups = len(plan)
    vmem = pl.BlockSpec(memory_space=pltpu.VMEM)
    hbm = pl.BlockSpec(memory_space=pl.ANY)
    dma = pltpu.SemaphoreType.DMA
    state = (heads, HEAD_DIM, HEAD_DIM)
    return pl.pallas_call(
        functools.partial(kernel, n, nh, plan),
        out_shape=jax.ShapeDtypeStruct((rows, own_cols), BF16),
        in_specs=[hbm, vmem, vmem, vmem],
        out_specs=hbm,
        scratch_shapes=[
            [pltpu.VMEM((lines, 2, 2, part_rows, count * HEAD_DIM), BF16) for _, _, count in plan],
            [pltpu.VMEM((part_rows, count * HEAD_DIM), BF16) for _, _, count in plan],
            pltpu.VMEM((2 * rows, width * nh), BF16),
            pltpu.VMEM((3, 2 * rows, cols), BF16),
            pltpu.VMEM((2 * rows, cols), BF16),
            pltpu.VMEM((2 * rows, plan[0][2] * HEAD_DIM), F32),
            pltpu.VMEM((2 * chunks,) + state, F32),
            pltpu.VMEM((2 * chunks,) + state, F32),
            pltpu.VMEM(state, F32),
            pltpu.VMEM(state, BF16),
            pltpu.VMEM((span,) + state, BF16),
            pltpu.VMEM((2, 1, rows), jnp.int32),
            pltpu.VMEM((2 * rows, HEAD_DIM), jnp.int32),
            pltpu.VMEM((8, HEAD_DIM), jnp.int32),
            pltpu.VMEM((span, 8, HEAD_DIM), jnp.int32),
            dma((groups,)), dma((groups,)),
            dma((groups, 2 * lines - 2)), dma((groups, 2 * lines - 2)),
            dma((groups, 2 * lines)), dma((groups, 2 * lines)),
            dma((nh - 1,)), dma((nh - 1,)), dma,
            dma((chunks,)), dma((chunks,)),
            dma((chunks, nh - 1)), dma((chunks, nh - 1)),
            dma((halves, span)), dma((halves, span)),
            dma((span,)), dma((span,)),
            dma, dma,
            dma((groups, chunks)), dma((groups, chunks)), dma((groups,)),
        ],
        compiler_params=pltpu.CompilerParams(
            collective_id=0, has_side_effects=True, vmem_limit_bytes=56 * 1024 * 1024
        ),
        cost_estimate=pl.CostEstimate(
            flops=2 * rows * width * nh * own_cols * 3,
            bytes_accessed=4 * rows * width, transcendentals=rows * own_cols,
        ),
    )(tokens, w_qkv, out_gain.reshape(1, own_cols), seg_ids.reshape(1, rows))


def solution(mesh):
    placed = (P("ctx", "head"), P(None, "ctx", "head"), P("head"), P("ctx"))
    sizes = (mesh.shape["ctx"], mesh.shape["head"])
    return jax.shard_map(
        functools.partial(per_device, *sizes),
        mesh=mesh, in_specs=placed, out_specs=P("ctx", "head"), check_vma=False,
    )
```

```python
import functools

import jax
import jax.numpy as jnp
from jax import lax
from jax.experimental import pallas as pl
from jax.experimental.pallas import tpu as pltpu
from jax.sharding import PartitionSpec as P

HEAD_DIM = 128
CHUNK = 256
MESH = pl.DeviceIdType.MESH
F32, BF16 = jnp.float32, jnp.bfloat16


def groups_of(heads):
    if heads % 4:
        return ((1, 0, heads), (2, 0, heads), (0, 0, heads))
    half = heads // 2
    first = tuple((which, 0, half) for which in (1, 2, 0))
    second = tuple((which, half, half) for which in (1, 2))
    return first + second + ((0, half, half // 2), (0, half + half // 2, half // 2))


def dot(left, right, dims=((1,), (0,))):
    return lax.dot_general(left, right, (dims, ((), ())), preferred_element_type=F32)


def kernel(
    n, nh, groups, tok_ref, w_ref, gain_ref, row_ref, out_ref, wbufs, wouts, tok, qkv, outs, local, incoming, state_out, state_got, row, col, tail_out, tail_got,
    x_send, x_recv, z_send, z_recv, y_send, y_recv,
    tok_send, tok_recv, tok_own, px_send, px_recv, ph_send, ph_recv,
    st_send, st_recv, tl_send, tl_recv, row_send, row_recv, out_send, out_recv, out_own,
):
    lines = n // 4
    pairs = n // 2
    span = n // 8
    rows, width = tok_ref.shape[0], tok_ref.shape[1]
    depth = n * w_ref.shape[1]
    all_heads = w_ref.shape[2] // 2 // HEAD_DIM
    heads = groups[0][2]
    halves = all_heads // heads
    chunks = rows // CHUNK
    last = len(groups) - 1
    ctx, head = lax.axis_index("ctx"), lax.axis_index("head")
    a, b, c = ctx // 4, (ctx // 2) % 2, ctx % 2
    pair = ctx // 2

    def place(a_, b_, c_):
        return (a_ * 4 + b_ * 2 + c_, head)

    def line_at(step):
        return lax.rem(a - step + lines, lines)

    for g, (which, first, count) in enumerate(groups):
        span_of = count * HEAD_DIM
        keep = pl.ds(pl.multiple_of((c * all_heads + first) * HEAD_DIM, 128), span_of)
        give = pl.ds(pl.multiple_of(((1 - c) * all_heads + first) * HEAD_DIM, 128), span_of)
        wbufs[g][a, b, c] = w_ref[which, :, keep]
        wouts[g][...] = w_ref[which, :, give]
    row[c] = row_ref[...]

    barrier = pltpu.get_barrier_semaphore()

    def greet(where):
        pl.semaphore_signal(barrier, inc=1, device_id=where, device_id_type=MESH)

    greet(place(a, b, 1 - c))
    greet(place(a, 1 - b, c))

    @pl.loop(1, lines)
    def _(d):
        greet(place(lax.rem(a + d, lines), b, c))

    @pl.loop(1, span + 1)
    def _(d):
        greet((lax.rem(pair + d, pairs) * 2 + c, head))
        greet((lax.rem(pair - d + pairs, pairs) * 2 + c, head))

    @pl.loop(1, nh)
    def _(d):
        greet((ctx, lax.rem(head + d, nh)))

    pl.semaphore_wait(barrier, 2 + (lines - 1) + 2 * span + (nh - 1))

    def remote(src, dst, send, recv, where):
        return pltpu.make_async_remote_copy(
            src_ref=src, dst_ref=dst, send_sem=send, recv_sem=recv,
            device_id=where, device_id_type=MESH,
        )

    def x_copy(g, c_):
        return remote(
            wouts[g], wbufs[g].at[a, b, c_], x_send.at[g], x_recv.at[g], place(a, b, 1 - c)
        )

    def z_copy(g, origin, far, way):
        slot = wbufs[g].at[origin, b, 1 - c if far else c]
        at = origin + (lines if far else 0)
        sent = at + (2 * lines if way > 0 else 0)
        to_line = lax.rem(a + way + lines, lines)
        return remote(slot, slot, z_send.at[g, sent], z_recv.at[g, at], place(to_line, b, c))

    def z_both(g, origin_of, far, act):
        for way in (1, -1):
            origin = origin_of(-way)

            @pl.when((origin >= 0) & (origin < lines) & (a + way >= 0) & (a + way < lines))
            def _():
                act(z_copy(g, lax.rem(origin + lines, lines), far, way))

    def y_copy(g, k, far, b_):
        slot = wbufs[g].at[line_at(k), b_, 1 - c if far else c]
        at = k + (lines if far else 0)
        return remote(slot, slot, y_send.at[g, at], y_recv.at[g, at], place(a, 1 - b, c))

    def features(of):
        return pl.ds(pl.multiple_of(of * width, 128), width)

    def own_rows(of):
        return pl.ds(pl.multiple_of(of * rows, CHUNK), rows)

    def piece(of, i):
        return pl.ds(pl.multiple_of(of * rows + i * CHUNK, CHUNK), CHUNK)

    def tok_copy(d, of, to):
        there = tok.at[own_rows(c), features(of)]
        return remote(tok_ref, there, tok_send.at[d - 1], tok_recv.at[d - 1], (ctx, to))

    def px_copy(i, of):
        return remote(
            tok_ref.at[pl.ds(i * CHUNK, CHUNK)], tok.at[piece(of, i), features(head)],
            px_send.at[i], px_recv.at[i], place(a, b, 1 - c),
        )

    def ph_copy(i, d, of, to):
        there = tok.at[piece(1 - c, i), features(of)]
        return remote(there, there, ph_send.at[i, d - 1], ph_recv.at[i, d - 1], (ctx, to))

    def state_copy(half, j):
        part = pl.ds(half * heads, heads)
        return remote(
            state_out.at[part], state_got.at[j, part], st_send.at[half, j], st_recv.at[half, j],
            (lax.rem(pair + j + 1, pairs) * 2 + c, head),
        )

    def tail_copy(j):
        return remote(
            tail_out, tail_got.at[j], tl_send.at[j], tl_recv.at[j],
            (lax.rem(pair + j + 1, pairs) * 2 + c, head),
        )

    def row_copy(c_):
        return remote(row.at[c_], row.at[c_], row_send, row_recv, place(a, b, 1 - c))

    def lanes_of(g):
        return pl.ds(groups[g][1] * HEAD_DIM, groups[g][2] * HEAD_DIM)

    def out_lanes(g, of):
        start = pl.multiple_of((of * all_heads + groups[g][1]) * HEAD_DIM, 128)
        return pl.ds(start, groups[g][2] * HEAD_DIM)

    def out_copy(g, i, of):
        at = pl.ds(pl.multiple_of(i * CHUNK, CHUNK), CHUNK)
        return remote(
            outs.at[piece(1 - c, i), lanes_of(g)], out_ref.at[at, out_lanes(g, of)],
            out_send.at[g, i], out_recv.at[g, i], place(a, b, 1 - c),
        )

    def out_keep(g):
        return pltpu.make_async_copy(
            outs.at[own_rows(c), lanes_of(g)], out_ref.at[:, out_lanes(g, c)], out_own.at[g]
        )

    def next_head(d):
        return lax.rem(head + d, nh)

    def prior_head(d):
        return lax.rem(head - d + nh, nh)

    def spread(g, far):
        y_copy(g, 0, far, b).start()

        z_both(g, lambda side: a, far, lambda copy: copy.start())

    def begin(g):
        if g <= last:
            x_copy(g, c).start()

    def own_part(g):
        if g <= last:
            spread(g, False)

    def pass_partner(g):
        if g <= last:
            x_copy(g, 1 - c).wait_recv()
            spread(g, True)

    def pass_lines(g):
        for far in (False, True):
            @pl.loop(1, lines if g <= last else 1)
            def _(d):
                for way in (1, -1):
                    origin = a - way * d

                    @pl.when((origin >= 0) & (origin < lines))
                    def _():
                        at = lax.rem(origin + lines, lines)
                        z_copy(g, at, far, way).wait_recv()

                        @pl.when((a + way >= 0) & (a + way < lines))
                        def _():
                            z_copy(g, at, far, way).start()

                        y_copy(g, lax.rem(a - origin + lines, lines), far, b).start()

    def finish(g):
        @pl.loop(0, lines)
        def _(d):
            for far in (False, True):
                y_copy(g, d, far, 1 - b).wait_recv()

    def project(g, of, i, height):
        which = groups[g][0]
        part = pl.ds(pl.multiple_of(of * rows + i * height, height), height)
        got = dot(tok[part, :], wbufs[g][...].reshape(depth, groups[g][2] * HEAD_DIM)).astype(BF16)
        if which < 2:
            wide = got.astype(F32)
            got = jnp.where(wide > 0.0, wide + 1.0, jnp.exp(jnp.minimum(wide, 0.0))).astype(BF16)
        qkv[which, part, lanes_of(g)] = got

    def project_own(g):
        @pl.loop(0, rows // 512)
        def _(i):
            project(g, c, i, 512)

    def ids_of(i):
        return row[i // chunks, :, (i % chunks) * CHUNK:(i % chunks + 1) * CHUNK]

    def least(ids):
        return jnp.min(ids, axis=1, keepdims=True)

    def most(ids):
        return jnp.max(ids, axis=1, keepdims=True)

    def own_states(half):
        for h in range(heads):
            at = half * heads + h
            lanes = pl.ds(at * HEAD_DIM, HEAD_DIM)
            state = jnp.zeros((HEAD_DIM, HEAD_DIM), F32)
            before = None
            for i in range(2 * chunks):
                part = pl.ds(i * CHUNK, CHUNK)
                first, tail = least(ids_of(i)), most(ids_of(i))
                if i > 0:
                    state = jnp.where(before == first, state, 0.0)
                local[i, at] = state
                keys = qkv[1, part, lanes]
                keys = jnp.where(col[part, 0:1] == tail, keys, jnp.zeros_like(keys))
                fresh = dot(keys, qkv[2, part, lanes], ((0,), (0,)))
                state = jnp.where(first == tail, state, 0.0) + fresh
                before = tail
            state_out[at] = state.astype(BF16)

        @pl.loop(0, span)
        def _(j):
            state_copy(half, j).start()

    def add_states(half):
        first = least(ids_of(0))
        own = range(half * heads, (half + 1) * heads)
        for at in own:
            incoming[at] = jnp.zeros((HEAD_DIM, HEAD_DIM), F32)

        @pl.loop(0, span)
        def _(j):
            if half == 0:
                tail_copy(j).wait_recv()
            state_copy(half, j).wait_recv()
            ids = tail_got[j][0:1, :] + jnp.where(pair > j, 0, -1000)
            linked = ids == first
            for at in own:
                incoming[at] += jnp.where(linked, state_got[j, at].astype(F32), 0.0)

        for i in range(2 * chunks):
            here = least(ids_of(i))
            for at in own:
                local[i, at] += jnp.where(here == first, incoming[at], 0.0)

    def attend(g, of, i):
        part = piece(of, i)
        ids_row = row[of, :, pl.ds(pl.multiple_of(i * CHUNK, CHUNK), CHUNK)]
        ids_col = col[part, 0:1]
        later = lax.broadcasted_iota(jnp.int32, (CHUNK, CHUNK), 0)
        sooner = lax.broadcasted_iota(jnp.int32, (CHUNK, CHUNK), 1)
        visible = (sooner <= later) & (ids_row == ids_col)
        reached = ids_col == least(ids_row)
        for at in range(groups[g][1], groups[g][1] + groups[g][2]):
            lanes = pl.ds(at * HEAD_DIM, HEAD_DIM)
            query = qkv[0, part, lanes]
            scores = dot(query, qkv[1, part, lanes], ((1,), (1,)))
            scores = jnp.where(visible, scores, 0.0).astype(BF16)
            total = dot(scores, qkv[2, part, lanes])
            prefix = dot(query, local[of * chunks + i, at].astype(BF16))
            total = total + jnp.where(reached, prefix, 0.0)
            scale = lax.rsqrt(jnp.mean(total * total, axis=1, keepdims=True) + 1e-05)
            gain = gain_ref[:, pl.ds(pl.multiple_of((c * all_heads + at) * HEAD_DIM, 128), HEAD_DIM)]
            outs[part, lanes] = (total * scale * gain).astype(BF16)

    def attend_partner(g, fresh):
        @pl.loop(0, rows // 512)
        def _(i):
            if fresh:
                project(g, 1 - c, i, 512)
            for part in range(512 // CHUNK):
                attend(g, 1 - c, i * (512 // CHUNK) + part)
            for part in range(512 // CHUNK):
                out_copy(g, i * (512 // CHUNK) + part, c).start()

    def attend_own(g, fresh):
        @pl.loop(0, rows // 512)
        def _(i):
            if fresh:
                project(g, c, i, 512)
            for part in range(512 // CHUNK):
                attend(g, c, i * (512 // CHUNK) + part)

        out_keep(g).start()

    def pass_piece(i):
        px_copy(i, 1 - c).wait_recv()

        @pl.loop(1, nh)
        def _(d):
            ph_copy(i, d, head, next_head(d)).start()

    def use_piece(i, of_groups):
        @pl.loop(1, nh)
        def _(d):
            ph_copy(i, d, prior_head(d), head).wait_recv()

        for g in of_groups:
            project(g, 1 - c, i, CHUNK)

    def project_pieces(g, count):
        @pl.loop(0, count)
        def _(i):
            project(g, 1 - c, i, CHUNK)

    def serve(g):
        begin(g + 3)
        if g + 1 < chunks:
            px_copy(g + 1, c).start()
        own_part(g + 2)
        pass_partner(g + 2)
        pass_lines(g + 1)

    for g in range(3):
        begin(g)
    own_part(0)

    @pl.loop(1, nh)
    def _(d):
        tok_copy(d, head, next_head(d)).start()

    own = pltpu.make_async_copy(tok_ref, tok.at[own_rows(c), features(head)], tok_own)
    own.start()
    row_copy(c).start()
    px_copy(0, c).start()
    pass_partner(0)
    own_part(1)
    pass_lines(0)
    pass_partner(1)
    row_copy(1 - c).wait_recv()
    tail_out[...] = jnp.broadcast_to(most(row[1]), tail_out.shape)

    @pl.loop(0, span)
    def _(j):
        tail_copy(j).start()

    for i in range(2 * chunks):
        col[pl.ds(i * CHUNK, CHUNK), :] = jnp.broadcast_to(ids_of(i), (HEAD_DIM, CHUNK)).T

    serve(0)
    own.wait()

    @pl.loop(1, nh)
    def _(d):
        tok_copy(d, prior_head(d), head).wait_recv()

    finish(0)
    project_own(0)
    serve(1)
    if halves == 1:
        for i in range(3, chunks):
            px_copy(i, c).start()
        finish(1)
        project_own(1)
        for i in range(chunks):
            pass_piece(i)
            use_piece(i, (0, 1))
        own_states(0)
        add_states(0)
        queries = (2,)
    else:
        for g in range(1, 4):
            if g > 1:
                serve(g)
            pass_piece(g - 1)
            finish(g)
            project_own(g)
            if g > 1:
                project_pieces(g, g - 1)
            use_piece(g - 1, range(g + 1))
        for i in range(3, chunks):
            if i > 3:
                px_copy(i, c).start()
            pass_piece(i)
        serve(4)
        for i in range(3, chunks):
            use_piece(i, range(4))
        own_states(0)
        add_states(0)
        attend_partner(2, False)
        serve(5)
        attend_own(2, False)
        finish(4)
        project_own(4)
        project_pieces(4, chunks)
        own_states(1)
        queries = (5, 6)
    for g in queries:
        finish(g)
        if g == 5:
            add_states(1)
        attend_partner(g, True)
        attend_own(g, True)

    for g in range(last + 1):
        x_copy(g, c).wait_send()

        @pl.loop(0, lines)
        def _(d):
            for far in (False, True):
                z_both(g, lambda side: a + side * d, far, lambda copy: copy.wait_send())

        @pl.loop(0, lines)
        def _(d):
            for far in (False, True):
                y_copy(g, d, far, b).wait_send()

    row_copy(c).wait_send()

    @pl.loop(1, nh)
    def _(d):
        tok_copy(d, head, next_head(d)).wait_send()

    for i in range(chunks):
        px_copy(i, c).wait_send()

        @pl.loop(1, nh)
        def _(d):
            ph_copy(i, d, head, next_head(d)).wait_send()

    @pl.loop(0, span)
    def _(j):
        tail_copy(j).wait_send()
        for half in range(halves):
            state_copy(half, j).wait_send()

    for g, (which, _, _) in enumerate(groups):
        if which == 0:
            out_keep(g).wait()

            @pl.loop(0, chunks)
            def _(i):
                out_copy(g, i, c).wait_send()
                out_copy(g, i, 1 - c).wait_recv()


def per_device(n, nh, tokens, w_qkv, out_gain, seg_ids):
    rows, width = tokens.shape
    part_rows, own_cols = w_qkv.shape[1:]
    cols = own_cols // 2
    heads = cols // HEAD_DIM
    plan = groups_of(heads)
    halves = heads // plan[0][2]
    lines, span, chunks = n // 4, n // 8, rows // CHUNK
    groups = len(plan)
    vmem = pl.BlockSpec(memory_space=pltpu.VMEM)
    hbm = pl.BlockSpec(memory_space=pl.ANY)
    dma = pltpu.SemaphoreType.DMA
    state = (heads, HEAD_DIM, HEAD_DIM)
    return pl.pallas_call(
        functools.partial(kernel, n, nh, plan),
        out_shape=jax.ShapeDtypeStruct((rows, own_cols), BF16),
        in_specs=[hbm, vmem, vmem, vmem],
        out_specs=hbm,
        scratch_shapes=[
            [pltpu.VMEM((lines, 2, 2, part_rows, count * HEAD_DIM), BF16) for _, _, count in plan],
            [pltpu.VMEM((part_rows, count * HEAD_DIM), BF16) for _, _, count in plan],
            pltpu.VMEM((2 * rows, width * nh), BF16),
            pltpu.VMEM((3, 2 * rows, cols), BF16),
            pltpu.VMEM((2 * rows, cols), BF16),
            pltpu.VMEM((2 * chunks,) + state, F32),
            pltpu.VMEM(state, F32),
            pltpu.VMEM(state, BF16),
            pltpu.VMEM((span,) + state, BF16),
            pltpu.VMEM((2, 1, rows), jnp.int32),
            pltpu.VMEM((2 * rows, HEAD_DIM), jnp.int32),
            pltpu.VMEM((8, HEAD_DIM), jnp.int32),
            pltpu.VMEM((span, 8, HEAD_DIM), jnp.int32),
            dma((groups,)), dma((groups,)),
            dma((groups, 4 * lines)), dma((groups, 2 * lines)),
            dma((groups, 2 * lines)), dma((groups, 2 * lines)),
            dma((nh - 1,)), dma((nh - 1,)), dma,
            dma((chunks,)), dma((chunks,)),
            dma((chunks, nh - 1)), dma((chunks, nh - 1)),
            dma((halves, span)), dma((halves, span)),
            dma((span,)), dma((span,)),
            dma, dma,
            dma((groups, chunks)), dma((groups, chunks)), dma((groups,)),
        ],
        compiler_params=pltpu.CompilerParams(
            collective_id=0, has_side_effects=True, vmem_limit_bytes=56 * 1024 * 1024
        ),
        cost_estimate=pl.CostEstimate(
            flops=2 * rows * width * nh * own_cols * 3,
            bytes_accessed=4 * rows * width, transcendentals=rows * own_cols,
        ),
    )(tokens, w_qkv, out_gain.reshape(1, own_cols), seg_ids.reshape(1, rows))


def solution(mesh):
    placed = (P("ctx", "head"), P(None, "ctx", "head"), P("head"), P("ctx"))
    sizes = (mesh.shape["ctx"], mesh.shape["head"])
    return jax.shard_map(
        functools.partial(per_device, *sizes),
        mesh=mesh, in_specs=placed, out_specs=P("ctx", "head"), check_vma=False,
    )
```
